32 devices in a mesh: seq: 16 (over z, x, core), head: 2 (over y).
Axes of the slice: x: 2, y: 2, z: 4, core: 2. Of those that a mesh axis runs over, the one named last changes fastest.
Arguments:
- queries: bfloat16 [2048, 8192], P('seq', 'head'), may hold values from -9 to 9
- image_kv: bfloat16 [2, 16384, 1024], P(None, ('seq', 'head')), may hold values from -9 to 9
- image_spans: int32 [16, 2], replicated, may hold values from 0 to 2048, as said below
- image_owner: int32 [16], replicated, may hold values from 0 to 15, as said below
- gate_logit: float32 [1], replicated, may hold values from 0.3 to 1
- grad_out: bfloat16 [2048, 8192], P('seq', 'head'), may hold values from -6 to 6
Outputs:
- attn_output: bfloat16 [2048, 8192], P('seq', 'head')
- grad_queries: bfloat16 [2048, 8192], P('seq', 'head')
- grad_image_kv: bfloat16 [2, 16384, 1024], P(None, ('seq', 'head'))
The draws below stay inside these ranges and needn't reach their ends.
Inputs may be any that keep to these rules, and one draw needn't show every extreme that they name: `image_owner`: A permutation: every row block of 1024 rows of image_kv holds exactly one image. For each image j, image_spans[j, 0] < image_spans[j, 1], and the span lies within text tokens 128 * image_owner[j] to 128 * (image_owner[j] + 3) - 1; the image held by block 0 is attended up to text token 383.
All inputs are finite; a program needn't handle non-finite values.
Results may differ from the reference program's by a relative error of at most 0.012.
The reference program's roundings to bfloat16 on the way (of `weights`, `grad_low`, `prob_low` and `score_grad`) count: a program that leaves them out, or rounds other values in their place, can miss the bound.
Values may be sent and summed in bfloat16 or wider, within the bound.
No kernel may reach another device: no remote copies, remote signals or barrier semaphores. Data moves between devices by JAX's collectives and lax.ppermute only.
A program may use at most 192 MiB of HBM per device.

```python
import math
import jax
import jax.numpy as jnp
from jax import lax

HEADS = 64
KVH = 8
HD = 128
TOK_DEV = 128
IMG_TOK = 1024
WIN = 3
NTOK = 2048
NIMG = 16
N_SEQ = 16


def layout_draw(key):
    owners = jax.random.permutation(jax.random.fold_in(key, 101), NIMG).astype(jnp.int32)
    offset = jax.random.randint(jax.random.fold_in(key, 102), (NIMG,), 0, TOK_DEV * (WIN - 1)).astype(jnp.int32)
    offset = jnp.where(owners == 0, offset % TOK_DEV, offset)
    span_start = jnp.minimum(owners * TOK_DEV + offset, NTOK - 1).astype(jnp.int32)
    span_limit = jnp.minimum((owners + WIN) * TOK_DEV, NTOK).astype(jnp.int32)
    extra_length = jax.random.randint(jax.random.fold_in(key, 103), (NIMG,), 0, span_limit - span_start).astype(jnp.int32)
    span_end = jnp.where(owners == 0, WIN * TOK_DEV, span_start + 1 + extra_length).astype(jnp.int32)
    return (owners, jnp.stack([span_start, span_end], axis=1).astype(jnp.int32))


def draw_image_owner(key, part):
    owners, spans_drawn = layout_draw(key)
    return owners


def draw_image_spans(key, part):
    owners, spans_drawn = layout_draw(key)
    return spans_drawn


def draw_queries(key, part):
    key = jax.random.fold_in(key, 7)
    base_draw = jnp.clip(jax.random.normal(key, (NTOK, HEADS * HD)), -6.0, 6.0)
    return base_draw.astype(jnp.bfloat16)


def draw_image_kv(key, part):
    key = jax.random.fold_in(key, 9)
    base_draw = jnp.clip(jax.random.normal(key, (2, NIMG * IMG_TOK, KVH * HD)), -6.0, 6.0)
    return base_draw.astype(jnp.bfloat16)


def steps_of(own_key, shape, cuts, least, high):
    factor_of, own = 1.0, jax.random.fold_in(own_key, 6)
    for position, shards_of in cuts:
        steps = jnp.exp(jax.random.uniform(jax.random.fold_in(own, position), (shards_of,), jnp.float32, least / len(cuts), high / len(cuts)))
        factor_of = factor_of * jnp.repeat(steps, shape[position] // shards_of).reshape([-1 if axis == position else 1 for axis in range(len(shape))])
    return factor_of


def noise(key, dims, width, reach, cuts=(), kind=jnp.bfloat16):
    entries = width * jax.random.normal(key, dims, jnp.float32)
    if cuts:
        entries = entries * steps_of(key, dims, cuts, -0.22, 0.18)
    return jnp.clip(entries, -reach, reach).astype(kind)


def setup_inputs(seed: int = 0) -> dict:
    splits = jax.random.split(jax.random.key(seed), 7)
    queries = draw_queries(jax.random.fold_in(splits[6], 71), 0)
    image_kv = draw_image_kv(jax.random.fold_in(splits[6], 71), 0)
    image_spans = draw_image_spans(jax.random.fold_in(splits[6], 71), 0)
    image_owner = draw_image_owner(jax.random.fold_in(splits[6], 71), 0)
    gate_logit = jnp.clip(jax.random.uniform(splits[4], (1,), jnp.float32, 0.3, 1.0), 0.3, 1.0)
    grad_out = noise(splits[5], (NTOK, HEADS * HD), 1.0, 6.0, ((0, 16), (1, 2)))
    return dict(queries=queries, image_kv=image_kv, image_spans=image_spans, image_owner=image_owner, gate_logit=gate_logit, grad_out=grad_out)


MASKED_VALUE = -1e+30

def rounded(array_in):
    return lax.optimization_barrier(array_in.astype(jnp.bfloat16)).astype(jnp.float32)

def reference(queries, image_kv, image_spans, image_owner, gate_logit, grad_out):
    group_size = HEADS // KVH
    inv_root = 1.0 / math.sqrt(HD)
    gate_gain = jnp.tanh(gate_logit[0])
    image_count = image_spans.shape[0]
    owner_match = image_owner[None, :] == jnp.arange(image_count, dtype=jnp.int32)[:, None]
    slot_start = lax.optimization_barrier(jnp.sum(jnp.where(owner_match, image_spans[None, :, 0], 0), axis=1)).astype(jnp.int32)
    slot_end = lax.optimization_barrier(jnp.sum(jnp.where(owner_match, image_spans[None, :, 1], 0), axis=1)).astype(jnp.int32)
    blocks = image_kv.reshape(2, image_count, IMG_TOK, KVH * HD)

    def one_shard(grad_sum, shard_id):
        row_start = shard_id * TOK_DEV
        query_rows = lax.dynamic_slice_in_dim(queries, row_start, TOK_DEV, 0).astype(jnp.float32)
        query_rows = query_rows.reshape(TOK_DEV, KVH, group_size, HD)
        cotangent = lax.dynamic_slice_in_dim(grad_out, row_start, TOK_DEV, 0).astype(jnp.float32)
        cotangent = cotangent.reshape(TOK_DEV, KVH, group_size, HD).transpose(1, 2, 0, 3)
        slot_ids = (shard_id - jnp.arange(WIN, dtype=jnp.int32)).astype(jnp.int32)
        slot_safe = jnp.maximum(slot_ids, 0).astype(jnp.int32)
        slot_match = slot_ids[:, None] == jnp.arange(image_count, dtype=jnp.int32)[None, :]
        starts = lax.optimization_barrier(jnp.sum(jnp.where(slot_match, slot_start[None, :], 0), axis=1))
        span_ends = lax.optimization_barrier(jnp.sum(jnp.where(slot_match, slot_end[None, :], 0), axis=1))
        positions = row_start + jnp.arange(TOK_DEV, dtype=jnp.int32)
        allowed = (positions[None, :] >= starts[:, None]) & (positions[None, :] < span_ends[:, None])
        key_mask = jnp.repeat(allowed.T, IMG_TOK, axis=1)
        window = jnp.take(blocks, slot_safe, axis=1).astype(jnp.float32).reshape(2, WIN * IMG_TOK, KVH, HD)
        key_rows = window[0]
        value_rows = window[1]
        scores = jnp.einsum('tkgd,jkd->kgtj', query_rows, key_rows) * inv_root
        visible = key_mask[None, None]
        row_max = lax.optimization_barrier(jnp.max(jnp.where(visible, scores, MASKED_VALUE), axis=-1, keepdims=True))
        any_row = jnp.any(key_mask, axis=-1)[None, None, :, None]
        row_max = jnp.where(any_row, row_max, 0.0)
        exp_scores = jnp.exp(jnp.where(visible, scores - row_max, MASKED_VALUE))
        row_total = lax.optimization_barrier(jnp.sum(exp_scores, axis=-1, keepdims=True))
        safe_total = jnp.where(row_total > 0, row_total, 1.0)
        weights = rounded(exp_scores)
        attended = jnp.einsum('kgtj,jkd->kgtd', weights, value_rows) / safe_total
        output_rows = rounded(gate_gain * attended).transpose(2, 0, 1, 3).reshape(TOK_DEV, HEADS * HD)
        attn_grad = gate_gain * cotangent
        grad_low = rounded(attn_grad)
        row_delta = lax.optimization_barrier(jnp.sum(attn_grad * attended, axis=-1, keepdims=True))
        probability = exp_scores / safe_total
        prob_low = rounded(probability)
        value_grad = jnp.einsum('kgtj,kgtd->jkd', prob_low, grad_low)
        prob_grad = jnp.einsum('kgtd,jkd->kgtj', grad_low, value_rows)
        score_grad = rounded(probability * (prob_grad - row_delta))
        query_grad = jnp.einsum('kgtj,jkd->tkgd', score_grad, key_rows) * inv_root
        query_grad = query_grad.astype(jnp.bfloat16).reshape(TOK_DEV, HEADS * HD)
        key_grad = jnp.einsum('kgtj,tkgd->jkd', score_grad, query_rows) * inv_root
        grad_window = jnp.stack([key_grad, value_grad]).reshape(2, WIN, IMG_TOK, KVH * HD)
        for offset in range(WIN):
            grad_sum = grad_sum.at[:, slot_safe[offset]].add(grad_window[:, offset])
        return (grad_sum, (output_rows.astype(jnp.bfloat16), query_grad))
    initial = jnp.zeros((2, image_count, IMG_TOK, KVH * HD), jnp.float32)
    grad_sum, stacked = lax.scan(one_shard, initial, jnp.arange(N_SEQ, dtype=jnp.int32))
    attn_output = stacked[0].reshape(NTOK, HEADS * HD)
    grad_queries = stacked[1].reshape(NTOK, HEADS * HD)
    grad_image_kv = grad_sum.astype(jnp.bfloat16).reshape(2, image_count * IMG_TOK, KVH * HD)
    return (attn_output, grad_queries, grad_image_kv)
```

```python
import functools, math
import jax
import jax.numpy as jnp
from jax import lax
from jax.experimental import pallas as pl
from jax.experimental.pallas import tpu as pltpu
from jax.sharding import PartitionSpec as P

HEADS = 64
KVH = 8
HD = 128
WIN = 3
GROUP = HEADS // KVH
INV_ROOT = 1.0 / math.sqrt(HD)
LOG2E = 1.4426950408889634
NEG = -1e30
BIG = 1e30
TOKC = 32
BLK = 256
NT = (((1,), (1,)), ((), ()))
NN = (((1,), (0,)), ((), ()))


def dot(a, b, dims=NN):
    return lax.dot_general(a, b, dims, preferred_element_type=jnp.float32)


def cuts_of(sizes):
    starts = [sum(sizes[:p]) for p in range(len(sizes))]
    return [(p, start, start + size) for p, (start, size) in enumerate(zip(starts, sizes))]


def blocks_of(sizes):
    return [
        (p, x - start, x, min(BLK, stop - x))
        for p, start, stop in cuts_of(sizes)
        for x in range(start, stop, BLK)
    ]


def attend_kernel(sizes, tok, carried, *refs):
    refs = list(refs)
    spans, gain_ref, q_ref, g_ref = refs[:4]
    del refs[:4]
    kv = [[refs.pop(0) for size in per] for per in sizes]
    del refs[:carried]
    out_ref, dq_ref = refs[:2]
    del refs[:2]
    grads = [[refs.pop(0) for size in per] for per in sizes]
    kt, vt, s, acc, m_ref, l_ref, o_ref, dqt_ref = refs
    width = GROUP * TOKC
    gain = gain_ref[0]
    blocks = [blocks_of(per) for per in sizes]

    for d in range(WIN):
        for p, start, stop in cuts_of(sizes[d]):
            kt[d, :, start:stop] = kv[d][p][0].T
            vt[d, :, start:stop] = kv[d][p][1].T
    acc[...] = jnp.zeros_like(acc)

    def chunk(c, carry):
        t0 = pl.multiple_of(c * TOKC, TOKC)
        toks = pl.ds(t0, TOKC)
        q = jnp.concatenate([q_ref[toks, g * HD : (g + 1) * HD] for g in range(GROUP)], axis=0)
        ag = gain * jnp.concatenate(
            [g_ref[toks, g * HD : (g + 1) * HD] for g in range(GROUP)], axis=0
        ).astype(jnp.float32)
        gl = ag.astype(jnp.bfloat16)
        at_tok = t0 + lax.rem(lax.broadcasted_iota(jnp.int32, (1, width), 1), TOKC)
        m_ref[...] = jnp.full_like(m_ref, NEG)
        l_ref[...] = jnp.zeros_like(l_ref)
        o_ref[...] = jnp.zeros_like(o_ref)
        dqt_ref[...] = jnp.zeros_like(dqt_ref)
        active = [(spans[1 + 2 * d] < t0 + TOKC) & (spans[2 + 2 * d] > t0) for d in range(WIN)]
        allowed = [(at_tok >= spans[1 + 2 * d]) & (at_tok < spans[2 + 2 * d]) for d in range(WIN)]

        for d in range(WIN):

            @pl.when(active[d])
            def _():
                top = jnp.full((8, width), NEG, jnp.float32)
                for p, r, x, blk in blocks[d]:
                    sc = dot(kv[d][p][0, r : r + blk, :], q, NT)
                    s[d, x : x + blk, :] = sc
                    top = jnp.maximum(top, jnp.max(sc.reshape(blk // 8, 8, width), axis=0))
                top = jnp.max(top, axis=0, keepdims=True)
                m_ref[...] = jnp.maximum(m_ref[...], jnp.where(allowed[d], top, NEG))

        for d in range(WIN):

            @pl.when(active[d])
            def _():
                shift = jnp.where(allowed[d], m_ref[...] * (INV_ROOT * LOG2E), BIG)
                total = jnp.zeros((8, width), jnp.float32)
                part = o_ref[...]
                for p, r, x, blk in blocks[d]:
                    e = jnp.exp2(s[d, x : x + blk, :] * (INV_ROOT * LOG2E) - shift)
                    s[d, x : x + blk, :] = e
                    total = total + jnp.sum(e.reshape(blk // 8, 8, width), axis=0)
                    part = part + dot(vt[d, :, x : x + blk], e.astype(jnp.bfloat16))
                o_ref[...] = part
                l_ref[...] += jnp.sum(total, axis=0, keepdims=True)

        l = l_ref[...]
        rl = 1.0 / jnp.where(l > 0, l, 1.0)
        att_t = o_ref[...] * rl
        delta = jnp.sum(ag.T * att_t, axis=0, keepdims=True)
        out = (gain * att_t).T.astype(jnp.bfloat16)
        for g in range(GROUP):
            out_ref[toks, g * HD : (g + 1) * HD] = out[g * TOKC : (g + 1) * TOKC]

        for d in range(WIN):

            @pl.when(active[d])
            def _():
                part = dqt_ref[...]
                for p, r, x, blk in blocks[d]:
                    dp = dot(kv[d][p][1, r : r + blk, :], gl, NT)
                    prob = s[d, x : x + blk, :] * rl
                    ds = (prob * (dp - delta)).astype(jnp.bfloat16)
                    acc[d, 1, x : x + blk, :] += dot(prob.astype(jnp.bfloat16), gl)
                    acc[d, 0, x : x + blk, :] += dot(ds, q)
                    part = part + dot(kt[d, :, x : x + blk], ds)
                dqt_ref[...] = part

        dq = (dqt_ref[...] * INV_ROOT).T.astype(jnp.bfloat16)
        for g in range(GROUP):
            dq_ref[toks, g * HD : (g + 1) * HD] = dq[g * TOKC : (g + 1) * TOKC]
        return carry

    lax.fori_loop(0, tok // TOKC, chunk, 0)

    for d in range(WIN):
        for p, start, stop in cuts_of(sizes[d]):
            grads[d][p][0] = (acc[d, 0, start:stop, :] * INV_ROOT).astype(grads[d][p].dtype)
            grads[d][p][1] = acc[d, 1, start:stop, :].astype(grads[d][p].dtype)


def attend(spans, gain, queries, grad_out, kv, carried, first, count, grad_types):
    tok = queries.shape[0]
    sizes = [[piece.shape[1] for piece in per] for per in kv]
    img = sum(sizes[0])
    width = GROUP * TOKC
    text = pl.BlockSpec((tok, GROUP * HD), lambda i, sp: (0, first + i))
    flat = [piece for per in kv for piece in per]

    def piece_spec(piece):
        shape = (2, piece.shape[1], HD)
        if piece.shape[2] == count * HD:
            return pl.BlockSpec(shape, lambda i, sp: (0, 0, i))
        return pl.BlockSpec(shape, lambda i, sp: (0, 0, sp[0] + first + i))

    grad_specs, grad_shapes = [], []
    for d in range(WIN):
        for size in sizes[d]:
            grad_specs.append(pl.BlockSpec((2, size, HD), lambda i, sp: (0, 0, i)))
            grad_shapes.append(jax.ShapeDtypeStruct((2, size, count * HD), grad_types[d]))
    text_shape = jax.ShapeDtypeStruct(queries.shape, jnp.bfloat16)
    n_in = 4 + len(flat)
    results = pl.pallas_call(
        functools.partial(attend_kernel, sizes, tok, len(carried)),
        out_shape=[text_shape, text_shape] + grad_shapes,
        grid_spec=pltpu.PrefetchScalarGridSpec(
            num_scalar_prefetch=1,
            grid=(count,),
            in_specs=[pl.BlockSpec(memory_space=pltpu.SMEM), text, text]
            + [piece_spec(piece) for piece in flat]
            + [pl.BlockSpec(memory_space=pl.ANY)] * len(carried),
            out_specs=[text, text] + grad_specs,
            scratch_shapes=[
                pltpu.VMEM((WIN, HD, img), jnp.bfloat16),
                pltpu.VMEM((WIN, HD, img), jnp.bfloat16),
                pltpu.VMEM((WIN, img, width), jnp.float32),
                pltpu.VMEM((WIN, 2, img, HD), jnp.float32),
                pltpu.VMEM((1, width), jnp.float32),
                pltpu.VMEM((1, width), jnp.float32),
                pltpu.VMEM((HD, width), jnp.float32),
                pltpu.VMEM((HD, width), jnp.float32),
            ],
        ),
        input_output_aliases={n_in + i: i for i in range(len(carried))},
        compiler_params=pltpu.CompilerParams(vmem_limit_bytes=40 * 2**20),
        cost_estimate=pl.CostEstimate(
            flops=12 * WIN * img * tok * GROUP * HD * count,
            bytes_accessed=count * 8 * 2**20,
            transcendentals=WIN * img * tok * GROUP * count,
        ),
    )(spans, gain, queries, grad_out, *flat, *carried)
    results = list(results)
    carried = tuple(results[:2])
    del results[:2]
    return carried, [[results.pop(0) for size in per] for per in sizes]


CHUNKS = 2


def shifted(shard, axis, by):
    count = lax.axis_size(axis)
    pairs = [(i, i + by) for i in range(count) if 0 <= i + by < count]
    return lax.ppermute(shard, axis, pairs)


def rotated(shard, axis, by):
    count = lax.axis_size(axis)
    return lax.ppermute(shard, axis, [(i, (i + by) % count) for i in range(count)])


def exchanged(shard, axis):
    return lax.ppermute(shard, axis, [(i, i ^ 1) for i in range(lax.axis_size(axis))])


def slot_bounds(image_spans, image_owner):
    image_count = image_spans.shape[0]
    owner_match = image_owner[None, :] == jnp.arange(image_count, dtype=jnp.int32)[:, None]
    slot_start = jnp.sum(jnp.where(owner_match, image_spans[None, :, 0], 0), axis=1)
    slot_end = jnp.sum(jnp.where(owner_match, image_spans[None, :, 1], 0), axis=1)
    return (slot_start, slot_end)


def shards(queries, image_kv, image_spans, image_owner, gate_logit, grad_out):
    head_count = lax.axis_size("head")
    my_head = lax.axis_index("head")
    my_shard = lax.axis_index("seq")
    odd = my_shard % 2 == 1
    tok_rows = queries.shape[0]
    rows = image_kv.shape[1]
    kv_local = KVH // head_count
    gain = jnp.tanh(gate_logit)
    slot_start, slot_end = slot_bounds(image_spans, image_owner)
    image_ids = jnp.arange(image_spans.shape[0], dtype=jnp.int32)
    bounds = [my_head * kv_local]
    for distance in range(WIN):
        slot_match = image_ids == my_shard - distance
        for slot in (slot_start, slot_end):
            at = jnp.sum(jnp.where(slot_match, slot - my_shard * tok_rows, 0))
            bounds.append(jnp.clip(at, 0, tok_rows))
    spans = jnp.stack(bounds).astype(jnp.int32)

    count = max(kv_local // CHUNKS, 1)
    firsts = range(0, kv_local, count)

    def columns(owner, first):
        return lax.dynamic_slice_in_dim(
            image_kv, (owner * kv_local + first) * HD, count * HD, axis=2
        )

    windows = []
    for first in firsts:
        own = [columns(my_head, first)]
        far = [shifted(own[0], "seq", 2)]
        for by in range(1, head_count):
            own.append(rotated(columns((my_head + by) % head_count, first), "head", by))
        for piece in own[1:]:
            far.append(shifted(piece, "seq", 2))
        near = exchanged(
            jnp.concatenate([jnp.where(odd, f, o) for f, o in zip(far, own)], axis=1), "seq"
        )
        windows.append([[image_kv] + own[1:], [near], far])

    carried = ()
    result = jnp.zeros_like(image_kv)
    for first, window in zip(firsts, windows):
        carried, grads = attend(
            spans,
            gain,
            queries,
            grad_out,
            window,
            carried,
            first,
            count,
            (jnp.float32, jnp.bfloat16, jnp.float32),
        )
        near_back = exchanged(grads[1][0], "seq").astype(jnp.float32)
        for by in reversed(range(head_count)):
            near_part = near_back[:, by * rows : (by + 1) * rows]
            leaving = grads[2][by] + jnp.where(odd, near_part, 0.0)
            kept = grads[0][by] + jnp.where(odd, 0.0, near_part)
            back = shifted(leaving.astype(jnp.bfloat16), "seq", -2).astype(jnp.float32)
            total = (kept + back).astype(jnp.bfloat16)
            if by:
                total = rotated(total, "head", -by)
            result = lax.dynamic_update_slice_in_dim(
                result, total, (((my_head + by) % head_count) * kv_local + first) * HD, axis=2
            )
    attn_output, grad_queries = carried
    return (attn_output, grad_queries, result)


def solution(mesh):
    placed = (P("seq", "head"), P(None, ("seq", "head"), None), P(), P(), P(), P("seq", "head"))
    return jax.shard_map(
        shards,
        mesh=mesh,
        in_specs=placed,
        out_specs=(P("seq", "head"), P("seq", "head"), P(None, ("seq", "head"), None)),
        check_vma=False,
    )
```

```python
import functools, math
import jax
import jax.numpy as jnp
from jax import lax
from jax.experimental import pallas as pl
from jax.experimental.pallas import tpu as pltpu
from jax.sharding import PartitionSpec as P

HEADS = 64
KVH = 8
HD = 128
WIN = 3
GROUP = HEADS // KVH
INV_ROOT = 1.0 / math.sqrt(HD)
LOG2E = 1.4426950408889634
NEG = -1e30
BIG = 1e30
GRAD_TYPES = (jnp.float32, jnp.bfloat16, jnp.float32)
TOKC = 64
BLK = 256
NT = (((1,), (1,)), ((), ()))
NN = (((1,), (0,)), ((), ()))


def dot(a, b, dims=NN):
    return lax.dot_general(a, b, dims, preferred_element_type=jnp.float32)


def cuts_of(sizes):
    starts = [sum(sizes[:p]) for p in range(len(sizes))]
    return [(p, start, start + size) for p, (start, size) in enumerate(zip(starts, sizes))]


def blocks_of(sizes):
    return [
        (p, x - start, x, min(BLK, stop - x))
        for p, start, stop in cuts_of(sizes)
        for x in range(start, stop, BLK)
    ]


def attend_kernel(sizes, grad_sizes, tok, carried, *refs):
    refs = list(refs)
    spans, gain_ref, q_ref, g_ref = refs[:4]
    del refs[:4]
    kv = [[refs.pop(0) for size in per] for per in sizes]
    del refs[:carried]
    out_ref, dq_ref = refs[:2]
    del refs[:2]
    grads = [[refs.pop(0) for size in per] for per in grad_sizes]
    kt, vt, s, acc, m_ref, l_ref, o_ref, dqt_ref = refs
    width = GROUP * TOKC
    gain = gain_ref[0]
    blocks = [blocks_of(per) for per in sizes]

    for d in range(WIN):
        for p, start, stop in cuts_of(sizes[d]):
            kt[d, :, start:stop] = kv[d][p][0].T
            vt[d, :, start:stop] = kv[d][p][1].T
    acc[...] = jnp.zeros_like(acc)

    def chunk(c, carry):
        t0 = pl.multiple_of(c * TOKC, TOKC)
        toks = pl.ds(t0, TOKC)
        q = jnp.concatenate([q_ref[toks, g * HD : (g + 1) * HD] for g in range(GROUP)], axis=0)
        ag = gain * jnp.concatenate(
            [g_ref[toks, g * HD : (g + 1) * HD] for g in range(GROUP)], axis=0
        ).astype(jnp.float32)
        gl = ag.astype(jnp.bfloat16)
        at_tok = t0 + lax.rem(lax.broadcasted_iota(jnp.int32, (1, width), 1), TOKC)
        m_ref[...] = jnp.full_like(m_ref, NEG)
        l_ref[...] = jnp.zeros_like(l_ref)
        o_ref[...] = jnp.zeros_like(o_ref)
        dqt_ref[...] = jnp.zeros_like(dqt_ref)
        active = [(spans[1 + 2 * d] < t0 + TOKC) & (spans[2 + 2 * d] > t0) for d in range(WIN)]
        allowed = [(at_tok >= spans[1 + 2 * d]) & (at_tok < spans[2 + 2 * d]) for d in range(WIN)]

        for d in range(WIN):

            @pl.when(active[d])
            def _():
                top = jnp.full((8, width), NEG, jnp.float32)
                for p, r, x, blk in blocks[d]:
                    sc = dot(kv[d][p][0, r : r + blk, :], q, NT)
                    s[d, x : x + blk, :] = sc
                    top = jnp.maximum(top, jnp.max(sc.reshape(blk // 8, 8, width), axis=0))
                top = jnp.max(top, axis=0, keepdims=True)
                m_ref[...] = jnp.maximum(m_ref[...], jnp.where(allowed[d], top, NEG))

        for d in range(WIN):

            @pl.when(active[d])
            def _():
                shift = jnp.where(allowed[d], m_ref[...] * (INV_ROOT * LOG2E), BIG)
                total = jnp.zeros((8, width), jnp.float32)
                part = o_ref[...]
                for p, r, x, blk in blocks[d]:
                    e = jnp.exp2(s[d, x : x + blk, :] * (INV_ROOT * LOG2E) - shift)
                    s[d, x : x + blk, :] = e
                    total = total + jnp.sum(e.reshape(blk // 8, 8, width), axis=0)
                    part = part + dot(vt[d, :, x : x + blk], e.astype(jnp.bfloat16))
                o_ref[...] = part
                l_ref[...] += jnp.sum(total, axis=0, keepdims=True)

        l = l_ref[...]
        rl = 1.0 / jnp.where(l > 0, l, 1.0)
        att_t = o_ref[...] * rl
        delta = jnp.sum(ag.T * att_t, axis=0, keepdims=True)
        out = (gain * att_t).T.astype(jnp.bfloat16)
        for g in range(GROUP):
            out_ref[toks, g * HD : (g + 1) * HD] = out[g * TOKC : (g + 1) * TOKC]

        for d in range(WIN):

            @pl.when(active[d])
            def _():
                part = dqt_ref[...]
                for p, r, x, blk in blocks[d]:
                    dp = dot(kv[d][p][1, r : r + blk, :], gl, NT)
                    prob = s[d, x : x + blk, :] * rl
                    ds = (prob * (dp - delta)).astype(jnp.bfloat16)
                    acc[d, 1, x : x + blk, :] += dot(prob.astype(jnp.bfloat16), gl)
                    acc[d, 0, x : x + blk, :] += dot(ds, q)
                    part = part + dot(kt[d, :, x : x + blk], ds)
                dqt_ref[...] = part

        dq = (dqt_ref[...] * INV_ROOT).T.astype(jnp.bfloat16)
        for g in range(GROUP):
            dq_ref[toks, g * HD : (g + 1) * HD] = dq[g * TOKC : (g + 1) * TOKC]
        return carry

    lax.fori_loop(0, tok // TOKC, chunk, 0)

    for d in range(WIN):
        for p, start, stop in cuts_of(grad_sizes[d]):
            grads[d][p][0] = (acc[d, 0, start:stop, :] * INV_ROOT).astype(grads[d][p].dtype)
            grads[d][p][1] = acc[d, 1, start:stop, :].astype(grads[d][p].dtype)


def attend(spans, gain, queries, grad_out, kv, text, grads, head, at, total, slot, grad_sizes):
    tok = queries.shape[0]
    sizes = [[piece.shape[1] for piece in per] for per in kv]
    img = sum(sizes[0])
    width = GROUP * TOKC
    text_spec = pl.BlockSpec((tok, GROUP * HD), lambda i, sp: (0, head))
    flat = [piece for per in kv for piece in per]

    def piece_spec(piece, local):
        shape = (2, piece.shape[1], HD)
        if local:
            return pl.BlockSpec(shape, lambda i, sp: (0, 0, sp[0] + head))
        return pl.BlockSpec(shape, lambda i, sp: (0, 0, at))

    grad_specs, grad_shapes = [], []
    for d in range(WIN):
        for size in grad_sizes[d]:
            grad_specs.append(pl.BlockSpec((2, size, HD), lambda i, sp: (0, 0, slot)))
            grad_shapes.append(jax.ShapeDtypeStruct((2, size, total * HD), GRAD_TYPES[d]))
    text_shape = jax.ShapeDtypeStruct(queries.shape, jnp.bfloat16)
    n_in = 4 + len(flat)
    carried = tuple(text) + tuple(grads)
    offset = 0 if text else 2
    results = pl.pallas_call(
        functools.partial(attend_kernel, sizes, grad_sizes, tok, len(carried)),
        out_shape=[text_shape, text_shape] + grad_shapes,
        grid_spec=pltpu.PrefetchScalarGridSpec(
            num_scalar_prefetch=1,
            grid=(1,),
            in_specs=[pl.BlockSpec(memory_space=pltpu.SMEM), text_spec, text_spec]
            + [piece_spec(piece, n == 0) for n, piece in enumerate(flat)]
            + [pl.BlockSpec(memory_space=pl.ANY)] * len(carried),
            out_specs=[text_spec, text_spec] + grad_specs,
            scratch_shapes=[
                pltpu.VMEM((WIN, HD, img), jnp.bfloat16),
                pltpu.VMEM((WIN, HD, img), jnp.bfloat16),
                pltpu.VMEM((WIN, img, width), jnp.float32),
                pltpu.VMEM((WIN, 2, img, HD), jnp.float32),
                pltpu.VMEM((1, width), jnp.float32),
                pltpu.VMEM((1, width), jnp.float32),
                pltpu.VMEM((HD, width), jnp.float32),
                pltpu.VMEM((HD, width), jnp.float32),
            ],
        ),
        input_output_aliases={n_in + i: i + offset for i in range(len(carried))},
        compiler_params=pltpu.CompilerParams(vmem_limit_bytes=40 * 2**20),
        cost_estimate=pl.CostEstimate(
            flops=WIN * img * tok * GROUP * HD,
            bytes_accessed=2**20,
            transcendentals=0,
        ),
    )(spans, gain, queries, grad_out, *flat, *carried)
    return tuple(results[:2]), tuple(results[2:])


def shifted(shard, axis, by):
    count = lax.axis_size(axis)
    pairs = [(i, i + by) for i in range(count) if 0 <= i + by < count]
    return lax.ppermute(shard, axis, pairs)


def rotated(shard, axis, by):
    count = lax.axis_size(axis)
    return lax.ppermute(shard, axis, [(i, (i + by) % count) for i in range(count)])


def exchanged(shard, axis):
    return lax.ppermute(shard, axis, [(i, i ^ 1) for i in range(lax.axis_size(axis))])


def after(values, earlier):
    return lax.optimization_barrier((values, earlier))[0]


def slot_bounds(image_spans, image_owner):
    image_count = image_spans.shape[0]
    owner_match = image_owner[None, :] == jnp.arange(image_count, dtype=jnp.int32)[:, None]
    slot_start = jnp.sum(jnp.where(owner_match, image_spans[None, :, 0], 0), axis=1)
    slot_end = jnp.sum(jnp.where(owner_match, image_spans[None, :, 1], 0), axis=1)
    return (slot_start, slot_end)


def shards(queries, image_kv, image_spans, image_owner, gate_logit, grad_out):
    head_count = lax.axis_size("head")
    my_head = lax.axis_index("head")
    my_shard = lax.axis_index("seq")
    odd = my_shard % 2 == 1
    tok_rows = queries.shape[0]
    rows = image_kv.shape[1]
    kv_local = KVH // head_count
    gain = jnp.tanh(gate_logit)
    slot_start, slot_end = slot_bounds(image_spans, image_owner)
    image_ids = jnp.arange(image_spans.shape[0], dtype=jnp.int32)
    bounds = [my_head * kv_local]
    for distance in range(WIN):
        slot_match = image_ids == my_shard - distance
        for slot in (slot_start, slot_end):
            at = jnp.sum(jnp.where(slot_match, slot - my_shard * tok_rows, 0))
            bounds.append(jnp.clip(at, 0, tok_rows))
    spans = jnp.stack(bounds).astype(jnp.int32)

    count = max(kv_local // 2, 1)
    groups = [list(range(count))] + [[head] for head in range(count, kv_local)]
    whole = [rows * head_count]
    pieces = [rows] * head_count

    def columns(owner, first):
        return lax.dynamic_slice_in_dim(
            image_kv, (owner * kv_local + first) * HD, count * HD, axis=2
        )

    arrivals = []
    before = ()
    for first in range(0, kv_local, count):
        own = [columns(my_head, first)]
        leaving = [columns((my_head + by) % head_count, first) for by in range(1, head_count)]
        own, leaving = after((own, leaving), before)
        own += [rotated(piece, "head", by + 1) for by, piece in enumerate(leaving)]
        far = [shifted(piece, "seq", 2) for piece in own]
        before = own[1:]
        arrivals.append((own, far))

    def window(chunk, earlier):
        own, far = arrivals[chunk]
        own, far = after((own, far), earlier)
        chosen = [jnp.where(odd, f, o) for f, o in zip(far, own)]
        near = exchanged(jnp.concatenate(chosen, axis=1), "seq")
        return [[image_kv] + own[1:], [near], far]

    def finish(result, pending, earlier):
        first, keeping, backs = pending
        totals = [None] * len(backs)
        for p in reversed(range(len(backs))):
            back = after(backs[p], earlier)
            totals[p] = (keeping[p] + back.astype(jnp.float32)).astype(jnp.bfloat16)
        if len(backs) < head_count:
            totals = [totals[0][:, start:stop] for p, start, stop in cuts_of(pieces)]
        waited = totals[-1]
        for by in reversed(range(head_count)):
            total = rotated(totals[by], "head", -by) if by else totals[by]
            at = (((my_head + by) % head_count) * kv_local + first) * HD
            result = lax.dynamic_update_slice_in_dim(result, total, at, axis=2)
        return result, waited

    text = ()
    result = jnp.zeros_like(image_kv)
    kv = window(0, before)
    hold = ()
    pending = None

    for g, group in enumerate(groups):
        last = g + 1 == len(groups)
        split = g == 0 or last
        cuts = pieces if split else whole
        grads = ()
        for slot, head in enumerate(group):
            text, grads = attend(
                after(spans, hold),
                gain,
                queries,
                grad_out,
                kv,
                text,
                grads,
                head,
                head % count,
                len(group),
                slot,
                (cuts, whole, cuts),
            )
            if g == 0 and slot == 0 and len(arrivals) > 1:
                hold = (arrivals[1][1][0], text)
        kept, near_grad, gone = grads[: len(cuts)], grads[len(cuts)], grads[len(cuts) + 1 :]
        if pending is not None:
            result, waited = finish(result, pending, near_grad)
            near_grad = after(near_grad, waited)
        near_back = exchanged(near_grad, "seq")
        if g == 0 and len(arrivals) > 1:
            kv = window(1, near_grad)
        leaving, backs, keeping = [], [], []
        for p, start, stop in reversed(cuts_of(cuts)):
            near_part = near_back[:, start:stop].astype(jnp.float32)
            leaving.append((gone[p] + jnp.where(odd, near_part, 0.0)).astype(jnp.bfloat16))
            keeping.append(kept[p] + jnp.where(odd, 0.0, near_part))
            backs.append(shifted(leaving[-1], "seq", -2))
        hold = leaving
        pending = (group[0], keeping[::-1], backs[::-1])
    result, waited = finish(result, pending, ())
    attn_output, grad_queries = text
    return (attn_output, grad_queries, result)


def solution(mesh):
    placed = (P("seq", "head"), P(None, ("seq", "head"), None), P(), P(), P(), P("seq", "head"))
    return jax.shard_map(
        shards,
        mesh=mesh,
        in_specs=placed,
        out_specs=(P("seq", "head"), P("seq", "head"), P(None, ("seq", "head"), None)),
        check_vma=False,
    )
```

```python
import functools, math
import jax
import jax.numpy as jnp
from jax import lax
from jax.experimental import pallas as pl
from jax.experimental.pallas import tpu as pltpu
from jax.sharding import PartitionSpec as P

HEADS = 64
KVH = 8
HD = 128
WIN = 3
GROUP = HEADS // KVH
INV_ROOT = 1.0 / math.sqrt(HD)
LOG2E = 1.4426950408889634
NEG = -1e30
BIG = 1e30
GRAD_TYPES = (jnp.float32, jnp.bfloat16, jnp.float32)
TOKC = 64
BLK = 256
NT = (((1,), (1,)), ((), ()))
NN = (((1,), (0,)), ((), ()))


def dot(a, b, dims=NN):
    return lax.dot_general(a, b, dims, preferred_element_type=jnp.float32)


def cuts_of(sizes):
    starts = [sum(sizes[:p]) for p in range(len(sizes))]
    return [(p, start, start + size) for p, (start, size) in enumerate(zip(starts, sizes))]


def blocks_of(sizes):
    return [
        (p, x - start, x, min(BLK, stop - x))
        for p, start, stop in cuts_of(sizes)
        for x in range(start, stop, BLK)
    ]


def attend_kernel(sizes, grad_sizes, tok, carried, *refs):
    refs = list(refs)
    spans, gain_ref, q_ref, g_ref = refs[:4]
    del refs[:4]
    kv = [[refs.pop(0) for size in per] for per in sizes]
    del refs[:carried]
    out_ref, dq_ref = refs[:2]
    del refs[:2]
    grads = [[refs.pop(0) for size in per] for per in grad_sizes]
    kt, vt, s, acc, m_ref, l_ref, o_ref, dqt_ref = refs
    width = GROUP * TOKC
    gain = gain_ref[0]
    blocks = [blocks_of(per) for per in sizes]

    for d in range(WIN):
        for p, start, stop in cuts_of(sizes[d]):
            kt[d, :, start:stop] = kv[d][p][0].T
            vt[d, :, start:stop] = kv[d][p][1].T
    acc[...] = jnp.zeros_like(acc)

    def chunk(c, carry):
        t0 = pl.multiple_of(c * TOKC, TOKC)
        toks = pl.ds(t0, TOKC)
        q = jnp.concatenate([q_ref[toks, g * HD : (g + 1) * HD] for g in range(GROUP)], axis=0)
        ag = gain * jnp.concatenate(
            [g_ref[toks, g * HD : (g + 1) * HD] for g in range(GROUP)], axis=0
        ).astype(jnp.float32)
        gl = ag.astype(jnp.bfloat16)
        at_tok = t0 + lax.rem(lax.broadcasted_iota(jnp.int32, (1, width), 1), TOKC)
        m_ref[...] = jnp.full_like(m_ref, NEG)
        l_ref[...] = jnp.zeros_like(l_ref)
        o_ref[...] = jnp.zeros_like(o_ref)
        dqt_ref[...] = jnp.zeros_like(dqt_ref)
        active = [(spans[1 + 2 * d] < t0 + TOKC) & (spans[2 + 2 * d] > t0) for d in range(WIN)]
        allowed = [(at_tok >= spans[1 + 2 * d]) & (at_tok < spans[2 + 2 * d]) for d in range(WIN)]

        for d in range(WIN):

            @pl.when(active[d])
            def _():
                top = jnp.full((8, width), NEG, jnp.float32)
                for p, r, x, blk in blocks[d]:
                    sc = dot(kv[d][p][0, r : r + blk, :], q, NT)
                    s[d, x : x + blk, :] = sc
                    top = jnp.maximum(top, jnp.max(sc.reshape(blk // 8, 8, width), axis=0))
                top = jnp.max(top, axis=0, keepdims=True)
                m_ref[...] = jnp.maximum(m_ref[...], jnp.where(allowed[d], top, NEG))

        for d in range(WIN):

            @pl.when(active[d])
            def _():
                shift = jnp.where(allowed[d], m_ref[...] * (INV_ROOT * LOG2E), BIG)
                total = jnp.zeros((8, width), jnp.float32)
                part = o_ref[...]
                for p, r, x, blk in blocks[d]:
                    e = jnp.exp2(s[d, x : x + blk, :] * (INV_ROOT * LOG2E) - shift)
                    s[d, x : x + blk, :] = e
                    total = total + jnp.sum(e.reshape(blk // 8, 8, width), axis=0)
                    part = part + dot(vt[d, :, x : x + blk], e.astype(jnp.bfloat16))
                o_ref[...] = part
                l_ref[...] += jnp.sum(total, axis=0, keepdims=True)

        l = l_ref[...]
        rl = 1.0 / jnp.where(l > 0, l, 1.0)
        att_t = o_ref[...] * rl
        delta = jnp.sum(ag.T * att_t, axis=0, keepdims=True)
        out = (gain * att_t).T.astype(jnp.bfloat16)
        for g in range(GROUP):
            out_ref[toks, g * HD : (g + 1) * HD] = out[g * TOKC : (g + 1) * TOKC]

        for d in range(WIN):

            @pl.when(active[d])
            def _():
                part = dqt_ref[...]
                for p, r, x, blk in blocks[d]:
                    dp = dot(kv[d][p][1, r : r + blk, :], gl, NT)
                    prob = s[d, x : x + blk, :] * rl
                    ds = (prob * (dp - delta)).astype(jnp.bfloat16)
                    acc[d, 1, x : x + blk, :] += dot(prob.astype(jnp.bfloat16), gl)
                    acc[d, 0, x : x + blk, :] += dot(ds, q)
                    part = part + dot(kt[d, :, x : x + blk], ds)
                dqt_ref[...] = part

        dq = (dqt_ref[...] * INV_ROOT).T.astype(jnp.bfloat16)
        for g in range(GROUP):
            dq_ref[toks, g * HD : (g + 1) * HD] = dq[g * TOKC : (g + 1) * TOKC]
        return carry

    lax.fori_loop(0, tok // TOKC, chunk, 0)

    for d in range(WIN):
        for p, start, stop in cuts_of(grad_sizes[d]):
            grads[d][p][0] = (acc[d, 0, start:stop, :] * INV_ROOT).astype(grads[d][p].dtype)
            grads[d][p][1] = acc[d, 1, start:stop, :].astype(grads[d][p].dtype)


def attend(spans, gain, queries, grad_out, kv, text, grads, head, at, total, slot, grad_sizes):
    tok = queries.shape[0]
    sizes = [[piece.shape[1] for piece in per] for per in kv]
    img = sum(sizes[0])
    width = GROUP * TOKC
    text_spec = pl.BlockSpec((tok, GROUP * HD), lambda i, sp: (0, head))
    flat = [piece for per in kv for piece in per]

    def piece_spec(piece, local):
        shape = (2, piece.shape[1], HD)
        if local:
            return pl.BlockSpec(shape, lambda i, sp: (0, 0, sp[0] + head))
        return pl.BlockSpec(shape, lambda i, sp: (0, 0, at))

    grad_specs, grad_shapes = [], []
    for d in range(WIN):
        for size in grad_sizes[d]:
            grad_specs.append(pl.BlockSpec((2, size, HD), lambda i, sp: (0, 0, slot)))
            grad_shapes.append(jax.ShapeDtypeStruct((2, size, total * HD), GRAD_TYPES[d]))
    text_shape = jax.ShapeDtypeStruct(queries.shape, jnp.bfloat16)
    n_in = 4 + len(flat)
    carried = tuple(text) + tuple(grads)
    offset = 0 if text else 2
    results = pl.pallas_call(
        functools.partial(attend_kernel, sizes, grad_sizes, tok, len(carried)),
        out_shape=[text_shape, text_shape] + grad_shapes,
        grid_spec=pltpu.PrefetchScalarGridSpec(
            num_scalar_prefetch=1,
            grid=(1,),
            in_specs=[pl.BlockSpec(memory_space=pltpu.SMEM), text_spec, text_spec]
            + [piece_spec(piece, n == 0) for n, piece in enumerate(flat)]
            + [pl.BlockSpec(memory_space=pl.ANY)] * len(carried),
            out_specs=[text_spec, text_spec] + grad_specs,
            scratch_shapes=[
                pltpu.VMEM((WIN, HD, img), jnp.bfloat16),
                pltpu.VMEM((WIN, HD, img), jnp.bfloat16),
                pltpu.VMEM((WIN, img, width), jnp.float32),
                pltpu.VMEM((WIN, 2, img, HD), jnp.float32),
                pltpu.VMEM((1, width), jnp.float32),
                pltpu.VMEM((1, width), jnp.float32),
                pltpu.VMEM((HD, width), jnp.float32),
                pltpu.VMEM((HD, width), jnp.float32),
            ],
        ),
        input_output_aliases={n_in + i: i + offset for i in range(len(carried))},
        compiler_params=pltpu.CompilerParams(vmem_limit_bytes=40 * 2**20),
        cost_estimate=pl.CostEstimate(
            flops=WIN * img * tok * GROUP * HD,
            bytes_accessed=2**20,
            transcendentals=0,
        ),
    )(spans, gain, queries, grad_out, *flat, *carried)
    return tuple(results[:2]), tuple(results[2:])


def shifted(shard, axis, by):
    count = lax.axis_size(axis)
    pairs = [(i, i + by) for i in range(count) if 0 <= i + by < count]
    return lax.ppermute(shard, axis, pairs)


def rotated(shard, axis, by):
    count = lax.axis_size(axis)
    return lax.ppermute(shard, axis, [(i, (i + by) % count) for i in range(count)])


def exchanged(shard, axis):
    return lax.ppermute(shard, axis, [(i, i ^ 1) for i in range(lax.axis_size(axis))])


def after(values, earlier):
    return lax.optimization_barrier((values, earlier))[0]


def slot_bounds(image_spans, image_owner):
    image_count = image_spans.shape[0]
    owner_match = image_owner[None, :] == jnp.arange(image_count, dtype=jnp.int32)[:, None]
    slot_start = jnp.sum(jnp.where(owner_match, image_spans[None, :, 0], 0), axis=1)
    slot_end = jnp.sum(jnp.where(owner_match, image_spans[None, :, 1], 0), axis=1)
    return (slot_start, slot_end)


def shards(queries, image_kv, image_spans, image_owner, gate_logit, grad_out):
    head_count = lax.axis_size("head")
    my_head = lax.axis_index("head")
    my_shard = lax.axis_index("seq")
    odd = my_shard % 2 == 1
    tok_rows = queries.shape[0]
    rows = image_kv.shape[1]
    kv_local = KVH // head_count
    gain = jnp.tanh(gate_logit)
    slot_start, slot_end = slot_bounds(image_spans, image_owner)
    image_ids = jnp.arange(image_spans.shape[0], dtype=jnp.int32)
    bounds = [my_head * kv_local]
    for distance in range(WIN):
        slot_match = image_ids == my_shard - distance
        for slot in (slot_start, slot_end):
            at = jnp.sum(jnp.where(slot_match, slot - my_shard * tok_rows, 0))
            bounds.append(jnp.clip(at, 0, tok_rows))
    spans = jnp.stack(bounds).astype(jnp.int32)

    count = max(kv_local // 2, 1)
    groups = [list(range(count))] + [[head] for head in range(count, kv_local)]
    whole = [rows * head_count]
    pieces = [rows] * head_count

    def columns(source, owner, first):
        start = (owner * kv_local + first) * HD
        return lax.dynamic_slice_in_dim(source, start, count * HD, axis=2)

    arrivals = []
    before = ()
    for first in range(0, kv_local, count):
        source = after(image_kv, before)
        own = [columns(source, my_head, first)]
        for by in range(1, head_count):
            leaving = columns(source, (my_head + by) % head_count, first)
            own.append(rotated(leaving, "head", by))
        far = [shifted(after(piece, spans) if by else piece, "seq", 2) for by, piece in enumerate(own)]
        before = own[1:]
        arrivals.append((own, far))

    def window(chunk, earlier):
        own, far = arrivals[chunk]
        own, far = after((own, far), earlier)
        chosen = [jnp.where(odd, f, o) for f, o in zip(far, own)]
        near = exchanged(jnp.concatenate(chosen, axis=1), "seq")
        return [[image_kv] + own[1:], [near], far]

    def finish(result, pending, earlier):
        first, keeping, backs = pending
        totals = [None] * len(backs)
        for p in reversed(range(len(backs))):
            back = after(backs[p], earlier)
            totals[p] = (keeping[p] + back.astype(jnp.float32)).astype(jnp.bfloat16)
        if len(backs) < head_count:
            totals = [totals[0][:, start:stop] for p, start, stop in cuts_of(pieces)]
        waited = totals[-1]
        for by in reversed(range(head_count)):
            total = rotated(totals[by], "head", -by) if by else totals[by]
            at = (((my_head + by) % head_count) * kv_local + first) * HD
            result = lax.dynamic_update_slice_in_dim(result, total, at, axis=2)
        return result, waited

    text = ()
    result = jnp.zeros_like(image_kv)
    kv = window(0, before)
    hold = ()
    pending = []

    for g, group in enumerate(groups):
        last = g + 1 == len(groups)
        split = last
        cuts = pieces if split else whole
        grads = ()
        for slot, head in enumerate(group):
            text, grads = attend(
                after(spans, hold),
                gain,
                queries,
                grad_out,
                kv,
                text,
                grads,
                head,
                head % count,
                len(group),
                slot,
                (cuts, whole, cuts),
            )
            if g == 0 and slot == 0 and len(arrivals) > 1:
                hold = (arrivals[1][1][0], text)
        kept, near_grad, gone = grads[: len(cuts)], grads[len(cuts)], grads[len(cuts) + 1 :]
        if len(pending) == 2:
            result, waited = finish(result, pending.pop(0), near_grad)
            near_grad = after(near_grad, waited)
        near_back = exchanged(near_grad, "seq")
        if last and len(pending) > 0:
            result, waited = finish(result, pending.pop(0), near_grad)
            near_back = after(near_back, waited)
        if g == 0 and len(arrivals) > 1:
            kv = window(1, near_grad)
        leaving, backs, keeping = [], [], []
        for p, start, stop in reversed(cuts_of(cuts)):
            near_part = near_back[:, start:stop].astype(jnp.float32)
            leaving.append((gone[p] + jnp.where(odd, near_part, 0.0)).astype(jnp.bfloat16))
            keeping.append(kept[p] + jnp.where(odd, 0.0, near_part))
            backs.append(shifted(leaving[-1], "seq", -2))
        hold = leaving
        pending.append((group[0], keeping[::-1], backs[::-1]))
    for n, item in enumerate(pending):
        result, waited = finish(result, item, leaving if n + 1 < len(pending) else ())
    attn_output, grad_queries = text
    return (attn_output, grad_queries, result)


def solution(mesh):
    placed = (P("seq", "head"), P(None, ("seq", "head"), None), P(), P(), P(), P("seq", "head"))
    return jax.shard_map(
        shards,
        mesh=mesh,
        in_specs=placed,
        out_specs=(P("seq", "head"), P("seq", "head"), P(None, ("seq", "head"), None)),
        check_vma=False,
    )
```

```python
import functools, math
import jax
import jax.numpy as jnp
from jax import lax
from jax.experimental import pallas as pl
from jax.experimental.pallas import tpu as pltpu
from jax.sharding import PartitionSpec as P

HEADS = 64
KVH = 8
HD = 128
WIN = 3
GROUP = HEADS // KVH
INV_ROOT = 1.0 / math.sqrt(HD)
LOG2E = 1.4426950408889634
NEG = -1e30
BIG = 1e30
VMEM_LIMIT = 36 * 2**20
GRAD_TYPES = (jnp.float32, jnp.bfloat16, jnp.float32)
BLK = 256
NT = (((1,), (1,)), ((), ()))
NN = (((1,), (0,)), ((), ()))


def dot(a, b, dims=NN):
    return lax.dot_general(a, b, dims, preferred_element_type=jnp.float32)


def cuts_of(sizes):
    starts = [sum(sizes[:p]) for p in range(len(sizes))]
    return [(p, start, start + size) for p, (start, size) in enumerate(zip(starts, sizes))]


def blocks_of(sizes):
    return [
        (p, x - start, x, min(BLK, stop - x))
        for p, start, stop in cuts_of(sizes)
        for x in range(start, stop, BLK)
    ]


def attend_kernel(sizes, grad_sizes, carried, place, *refs):
    head, at, slot = place
    refs = list(refs)
    spans, gain_ref, q_ref, g_ref = refs[:4]
    del refs[:4]
    kv = [[refs.pop(0) for size in per] for per in sizes]
    del refs[:carried]
    out_ref, dq_ref = refs[:2]
    del refs[:2]
    grads = [[refs.pop(0) for size in per] for per in grad_sizes]
    kt, vt, s, m_ref, l_ref, o_ref, dqt_ref = refs
    tok = q_ref.shape[0]
    width = GROUP * tok
    gain = gain_ref[0]
    blocks = [blocks_of(per) for per in sizes]
    cols = slice(at * HD, (at + 1) * HD)
    slots = slice(slot * HD, (slot + 1) * HD)
    text = [slice((head * GROUP + g) * HD, (head * GROUP + g + 1) * HD) for g in range(GROUP)]

    q = jnp.concatenate([q_ref[:, cut] for cut in text], axis=0)
    ag = gain * jnp.concatenate([g_ref[:, cut] for cut in text], axis=0).astype(jnp.float32)
    gl = ag.astype(jnp.bfloat16)
    at_tok = lax.rem(lax.broadcasted_iota(jnp.int32, (1, width), 1), tok)
    m_ref[...] = jnp.full_like(m_ref, NEG)
    l_ref[...] = jnp.zeros_like(l_ref)
    o_ref[...] = jnp.zeros_like(o_ref)
    dqt_ref[...] = jnp.zeros_like(dqt_ref)
    active = [spans[2 * d + 1] > spans[2 * d] for d in range(WIN)]
    allowed = [(at_tok >= spans[2 * d]) & (at_tok < spans[2 * d + 1]) for d in range(WIN)]

    for d in range(WIN):

        @pl.when(active[d])
        def _():
            top = jnp.full((8, width), NEG, jnp.float32)
            for p, r, x, blk in blocks[d]:
                sc = dot(kv[d][p][0, r : r + blk, cols], q, NT)
                s[d, x : x + blk, :] = sc
                top = jnp.maximum(top, jnp.max(sc.reshape(blk // 8, 8, width), axis=0))
                kt[d, :, x : x + blk] = kv[d][p][0, r : r + blk, cols].T
                vt[d, :, x : x + blk] = kv[d][p][1, r : r + blk, cols].T
            top = jnp.max(top, axis=0, keepdims=True)
            m_ref[...] = jnp.maximum(m_ref[...], jnp.where(allowed[d], top, NEG))

    for d in range(WIN):

        @pl.when(active[d])
        def _():
            shift = jnp.where(allowed[d], m_ref[...] * (INV_ROOT * LOG2E), BIG)
            total = jnp.zeros((8, width), jnp.float32)
            for p, r, x, blk in blocks[d]:
                e = jnp.exp2(s[d, x : x + blk, :] * (INV_ROOT * LOG2E) - shift)
                s[d, x : x + blk, :] = e
                total = total + jnp.sum(e.reshape(blk // 8, 8, width), axis=0)
                o_ref[...] += dot(vt[d, :, x : x + blk], e.astype(jnp.bfloat16))
            l_ref[...] += jnp.sum(total, axis=0, keepdims=True)

    l = l_ref[...]
    rl = 1.0 / jnp.where(l > 0, l, 1.0)
    att_t = o_ref[...] * rl
    delta = jnp.sum(ag.T * att_t, axis=0, keepdims=True)
    out = (gain * att_t).T.astype(jnp.bfloat16)
    for g in range(GROUP):
        out_ref[:, g * HD : (g + 1) * HD] = out[g * tok : (g + 1) * tok]

    for d in range(WIN):
        grad_cuts = cuts_of(grad_sizes[d])

        @pl.when(active[d])
        def _():
            for p, r, x, blk in blocks[d]:
                c, start, stop = [cut for cut in grad_cuts if cut[1] <= x < cut[2]][0]
                rows = slice(x - start, x - start + blk)
                into = grads[d][c]
                dp = dot(kv[d][p][1, r : r + blk, cols], gl, NT)
                prob = s[d, x : x + blk, :] * rl
                ds = (prob * (dp - delta)).astype(jnp.bfloat16)
                into[1, rows, slots] = dot(prob.astype(jnp.bfloat16), gl).astype(into.dtype)
                into[0, rows, slots] = (dot(ds, q) * INV_ROOT).astype(into.dtype)
                dqt_ref[...] += dot(kt[d, :, x : x + blk], ds)

        @pl.when(jnp.logical_not(active[d]))
        def _():
            for c, start, stop in grad_cuts:
                into = grads[d][c]
                into[:, :, slots] = jnp.zeros((2, stop - start, HD), into.dtype)

    dq = (dqt_ref[...] * INV_ROOT).T.astype(jnp.bfloat16)
    for g in range(GROUP):
        dq_ref[:, g * HD : (g + 1) * HD] = dq[g * tok : (g + 1) * tok]


def attend(spans, gain, queries, grad_out, kv, text, grads, head, at, total, slot, grad_sizes):
    tok = queries.shape[0]
    sizes = [[piece.shape[1] for piece in per] for per in kv]
    img = sum(sizes[0])
    width = GROUP * tok
    flat = [piece for per in kv for piece in per]
    vmem = pl.BlockSpec(memory_space=pltpu.VMEM)
    smem = pl.BlockSpec(memory_space=pltpu.SMEM)
    hbm = pl.BlockSpec(memory_space=pl.ANY)
    text_spec = pl.BlockSpec((tok, GROUP * HD), lambda i: (0, head))
    grad_shapes = [
        jax.ShapeDtypeStruct((2, size, total * HD), GRAD_TYPES[d])
        for d in range(WIN)
        for size in grad_sizes[d]
    ]
    text_shape = jax.ShapeDtypeStruct(queries.shape, jnp.bfloat16)
    n_in = 4 + len(flat)
    carried = tuple(text) + tuple(grads)
    offset = 0 if text else 2
    results = pl.pallas_call(
        functools.partial(attend_kernel, sizes, grad_sizes, len(carried), (head, at, slot)),
        out_shape=[text_shape, text_shape] + grad_shapes,
        grid=(1,),
        in_specs=[smem, smem, vmem, vmem]
        + [vmem] * len(flat)
        + [hbm] * len(text)
        + [vmem] * len(grads),
        out_specs=[text_spec] * 2 + [vmem] * len(grad_shapes),
        scratch_shapes=[
            pltpu.VMEM((WIN, HD, img), jnp.bfloat16),
            pltpu.VMEM((WIN, HD, img), jnp.bfloat16),
            pltpu.VMEM((WIN, img, width), jnp.float32),
            pltpu.VMEM((1, width), jnp.float32),
            pltpu.VMEM((1, width), jnp.float32),
            pltpu.VMEM((HD, width), jnp.float32),
            pltpu.VMEM((HD, width), jnp.float32),
        ],
        input_output_aliases={n_in + i: i + offset for i in range(len(carried))},
        compiler_params=pltpu.CompilerParams(vmem_limit_bytes=VMEM_LIMIT),
        cost_estimate=pl.CostEstimate(
            flops=WIN * img * tok * GROUP * HD, bytes_accessed=2**20, transcendentals=0
        ),
    )(spans, gain, queries, grad_out, *flat, *carried)
    return tuple(results[:2]), tuple(results[2:])


def shifted(shard, axis, by):
    count = lax.axis_size(axis)
    pairs = [(i, i + by) for i in range(count) if 0 <= i + by < count]
    return lax.ppermute(shard, axis, pairs)


def rotated(shard, axis, by):
    count = lax.axis_size(axis)
    return lax.ppermute(shard, axis, [(i, (i + by) % count) for i in range(count)])


def exchanged(shard, axis):
    return lax.ppermute(shard, axis, [(i, i ^ 1) for i in range(lax.axis_size(axis))])


def after(values, earlier):
    return lax.optimization_barrier((values, earlier))[0]


def slot_bounds(image_spans, image_owner):
    image_count = image_spans.shape[0]
    owner_match = image_owner[None, :] == jnp.arange(image_count, dtype=jnp.int32)[:, None]
    slot_start = jnp.sum(jnp.where(owner_match, image_spans[None, :, 0], 0), axis=1)
    slot_end = jnp.sum(jnp.where(owner_match, image_spans[None, :, 1], 0), axis=1)
    return (slot_start, slot_end)


def shards(queries, image_kv, image_spans, image_owner, gate_logit, grad_out):
    head_count = lax.axis_size("head")
    my_head = lax.axis_index("head")
    my_shard = lax.axis_index("seq")
    odd = my_shard % 2 == 1
    tok_rows = queries.shape[0]
    rows = image_kv.shape[1]
    kv_local = KVH // head_count
    gain = jnp.tanh(gate_logit)
    slot_start, slot_end = slot_bounds(image_spans, image_owner)
    image_ids = jnp.arange(image_spans.shape[0], dtype=jnp.int32)
    bounds = []
    for distance in range(WIN):
        slot_match = image_ids == my_shard - distance
        for slot in (slot_start, slot_end):
            at = jnp.sum(jnp.where(slot_match, slot - my_shard * tok_rows, 0))
            bounds.append(jnp.clip(at, 0, tok_rows))
    spans = jnp.stack(bounds).astype(jnp.int32)

    count = max(kv_local // 2, 1)
    groups = [list(range(count))] + [[head] for head in range(count, kv_local)]
    whole = [rows * head_count]
    pieces = [rows] * head_count

    def columns(source, owner, first):
        start = (owner * kv_local + first) * HD
        return lax.dynamic_slice_in_dim(source, start, count * HD, axis=2)

    arrivals = []
    before = ()
    for first in range(0, kv_local, count):
        source = after(image_kv, before)
        slices = [
            columns(source, (my_head + by) % head_count, first) for by in range(head_count)
        ]
        if not arrivals:
            own = slices[:1]
            own += [rotated(slices[by], "head", by) for by in range(1, head_count)]
            before = spans
            arrivals.append(own)
        else:
            early = slices
            slices = after(slices, arrivals[0][1:])
            own = slices[:1]
            own += [rotated(slices[by], "head", by) for by in range(1, head_count)]
            arrivals.append(own)
    if len(arrivals) == 1:
        early = ()
    far = [
        shifted(after(piece, (spans, early)) if by else piece, "seq", 2)
        for by, piece in enumerate(arrivals[0])
    ]
    near = [jnp.where(odd, f, o) for f, o in zip(far, arrivals[0])]
    near = jnp.concatenate(after(near, arrivals[-1][1:]), axis=1)
    kv = [arrivals[0], [exchanged(near, "seq")], far]
    if len(arrivals) > 1:
        next_own = jnp.concatenate(arrivals[1], axis=1)
        next_far = shifted(next_own, "seq", 2)

    def finish(result, pending, earlier):
        first, keeping, backs = pending
        totals = [None] * len(backs)
        for p in reversed(range(len(backs))):
            back = after(backs[p], earlier)
            totals[p] = (keeping[p] + back.astype(jnp.float32)).astype(jnp.bfloat16)
        if len(backs) < head_count:
            totals = [totals[0][:, start:stop] for p, start, stop in cuts_of(pieces)]
        waited = totals[-1]
        for by in reversed(range(head_count)):
            total = rotated(totals[by], "head", -by) if by else totals[by]
            at = (((my_head + by) % head_count) * kv_local + first) * HD
            result = lax.dynamic_update_slice_in_dim(result, total, at, axis=2)
        return result, waited

    text = ()
    result = jnp.zeros_like(image_kv)
    hold = ()
    pending = []

    for g, group in enumerate(groups):
        last = g + 1 == len(groups)
        split = last
        cuts = pieces if split else whole
        grads = ()
        for slot, head in enumerate(group):
            text, grads = attend(
                after(spans, hold),
                gain,
                queries,
                grad_out,
                kv,
                text,
                grads,
                head,
                head % count,
                len(group),
                slot,
                (cuts, whole, cuts),
            )
            if g == 0 and slot == 0 and len(arrivals) > 1:
                hold = text
        kept, near_grad, gone = grads[: len(cuts)], grads[len(cuts)], grads[len(cuts) + 1 :]
        if len(pending) == 2:
            result, waited = finish(result, pending.pop(0), near_grad)
            near_grad = after(near_grad, waited)
        near_back = exchanged(near_grad, "seq")
        if last and len(pending) > 0:
            result, waited = finish(result, pending.pop(0), near_grad)
            near_back = after(near_back, waited)
        if g == 0 and len(arrivals) > 1:
            next_own, next_far = after((next_own, next_far), near_grad)
            kv = [[next_own], [exchanged(jnp.where(odd, next_far, next_own), "seq")], [next_far]]
        leaving, backs, keeping = [], [], []
        for p, start, stop in reversed(cuts_of(cuts)):
            near_part = near_back[:, start:stop].astype(jnp.float32)
            leaving.append((gone[p] + jnp.where(odd, near_part, 0.0)).astype(jnp.bfloat16))
            keeping.append(kept[p] + jnp.where(odd, 0.0, near_part))
            backs.append(shifted(leaving[-1], "seq", -2))
        hold = leaving
        pending.append((group[0], keeping[::-1], backs[::-1]))
    for n, item in enumerate(pending):
        result, waited = finish(result, item, leaving if n + 1 < len(pending) else ())
    attn_output, grad_queries = text
    return (attn_output, grad_queries, result)


def solution(mesh):
    placed = (P("seq", "head"), P(None, ("seq", "head"), None), P(), P(), P(), P("seq", "head"))
    return jax.shard_map(
        shards,
        mesh=mesh,
        in_specs=placed,
        out_specs=(P("seq", "head"), P("seq", "head"), P(None, ("seq", "head"), None)),
        check_vma=False,
    )
```

```python
import functools, math
import jax
import jax.numpy as jnp
from jax import lax
from jax.experimental import pallas as pl
from jax.experimental.pallas import tpu as pltpu
from jax.sharding import PartitionSpec as P

HEADS = 64
KVH = 8
HD = 128
WIN = 3
GROUP = HEADS // KVH
INV_ROOT = 1.0 / math.sqrt(HD)
LOG2E = 1.4426950408889634
NEG = -1e30
BIG = 1e30
VMEM_LIMIT = 36 * 2**20
GRAD_TYPES = (jnp.float32, jnp.bfloat16, jnp.float32)
BLK = 512
UNROLLED = 2
NT = (((1,), (1,)), ((), ()))
NN = (((1,), (0,)), ((), ()))


def dot(a, b, dims=NN):
    return lax.dot_general(a, b, dims, preferred_element_type=jnp.float32)


def cuts_of(sizes):
    starts = [sum(sizes[:p]) for p in range(len(sizes))]
    return [(p, start, start + size) for p, (start, size) in enumerate(zip(starts, sizes))]


def over_blocks(sizes, body):
    for p, start, stop in cuts_of(sizes):
        blk = min(BLK, stop - start)
        if stop - start <= UNROLLED * blk:
            for r in range(0, stop - start, blk):
                body(p, pl.ds(r, blk), pl.ds(start + r, blk))
        else:

            @pl.loop(0, (stop - start) // blk)
            def _(n):
                r = pl.multiple_of(n * blk, blk)
                body(p, pl.ds(r, blk), pl.ds(pl.multiple_of(start + r, blk), blk))


def attend_kernel(sizes, carried, place, *refs):
    head, at = place
    step = pl.program_id(0)
    refs = list(refs)
    spans, gain_ref, q_ref, g_ref = refs[:4]
    del refs[:4]
    kv = [[refs.pop(0) for size in per] for per in sizes]
    del refs[:carried]
    out_ref, dq_ref = refs[:2]
    del refs[:2]
    grads = [refs.pop(0) for d in range(WIN)]
    kt, vt, s, top, total, m_ref, l_ref, o_ref, dqt_ref = refs
    tok = q_ref.shape[0]
    width = GROUP * tok
    gain = gain_ref[0]

    def column(first):
        return pl.ds(pl.multiple_of(first * HD, HD), HD)

    cols = column(at + step)
    slots = column(step)
    text = [column((head + step) * GROUP + g) for g in range(GROUP)]

    q = jnp.concatenate([q_ref[:, cut] for cut in text], axis=0)
    ag = gain * jnp.concatenate([g_ref[:, cut] for cut in text], axis=0).astype(jnp.float32)
    gl = ag.astype(jnp.bfloat16)
    at_tok = lax.rem(lax.broadcasted_iota(jnp.int32, (1, width), 1), tok)
    m_ref[...] = jnp.full_like(m_ref, NEG)
    l_ref[...] = jnp.zeros_like(l_ref)
    o_ref[...] = jnp.zeros_like(o_ref)
    dqt_ref[...] = jnp.zeros_like(dqt_ref)
    active = [spans[2 * d + 1] > spans[2 * d] for d in range(WIN)]
    allowed = [(at_tok >= spans[2 * d]) & (at_tok < spans[2 * d + 1]) for d in range(WIN)]

    for d in range(WIN):

        @pl.when(active[d])
        def _():
            top[...] = jnp.full_like(top, NEG)

            def body(p, rows, image_rows):
                sc = dot(kv[d][p][0, rows, cols], q, NT)
                s[d, image_rows, :] = sc
                top[...] = jnp.maximum(top[...], jnp.max(sc.reshape(-1, 8, width), axis=0))
                kt[d, :, image_rows] = kv[d][p][0, rows, cols].T
                vt[d, :, image_rows] = kv[d][p][1, rows, cols].T

            over_blocks(sizes[d], body)
            highest = jnp.max(top[...], axis=0, keepdims=True)
            m_ref[...] = jnp.maximum(m_ref[...], jnp.where(allowed[d], highest, NEG))

    for d in range(WIN):

        @pl.when(active[d])
        def _():
            shift = jnp.where(allowed[d], m_ref[...] * (INV_ROOT * LOG2E), BIG)
            total[...] = jnp.zeros_like(total)

            def body(p, rows, image_rows):
                e = jnp.exp2(s[d, image_rows, :] * (INV_ROOT * LOG2E) - shift)
                s[d, image_rows, :] = e
                total[...] += jnp.sum(e.reshape(-1, 8, width), axis=0)
                o_ref[...] += dot(vt[d, :, image_rows], e.astype(jnp.bfloat16))

            over_blocks(sizes[d], body)
            l_ref[...] += jnp.sum(total[...], axis=0, keepdims=True)

    l = l_ref[...]
    rl = 1.0 / jnp.where(l > 0, l, 1.0)
    att_t = o_ref[...] * rl
    delta = jnp.sum(ag.T * att_t, axis=0, keepdims=True)
    out = (gain * att_t).T.astype(jnp.bfloat16)
    for g in range(GROUP):
        out_ref[:, g * HD : (g + 1) * HD] = out[g * tok : (g + 1) * tok]

    for d in range(WIN):
        into = grads[d]

        @pl.when(active[d])
        def _():
            def body(p, rows, image_rows):
                dp = dot(kv[d][p][1, rows, cols], gl, NT)
                prob = s[d, image_rows, :] * rl
                ds = (prob * (dp - delta)).astype(jnp.bfloat16)
                into[1, image_rows, slots] = dot(prob.astype(jnp.bfloat16), gl).astype(into.dtype)
                into[0, image_rows, slots] = (dot(ds, q) * INV_ROOT).astype(into.dtype)
                dqt_ref[...] += dot(kt[d, :, image_rows], ds)

            over_blocks(sizes[d], body)

        @pl.when(jnp.logical_not(active[d]))
        def _():
            into[:, :, slots] = jnp.zeros((*into.shape[:2], HD), into.dtype)

    dq = (dqt_ref[...] * INV_ROOT).T.astype(jnp.bfloat16)
    for g in range(GROUP):
        dq_ref[:, g * HD : (g + 1) * HD] = dq[g * tok : (g + 1) * tok]


def attend(spans, gain, queries, grad_out, kv, text, head, at, heads):
    tok = queries.shape[0]
    sizes = [[piece.shape[1] for piece in per] for per in kv]
    img = sum(sizes[0])
    width = GROUP * tok
    flat = [piece for per in kv for piece in per]
    vmem = pl.BlockSpec(memory_space=pltpu.VMEM)
    smem = pl.BlockSpec(memory_space=pltpu.SMEM)
    hbm = pl.BlockSpec(memory_space=pl.ANY)
    text_spec = pl.BlockSpec((tok, GROUP * HD), lambda i: (0, head + i))
    grad_shapes = [
        jax.ShapeDtypeStruct((2, img, heads * HD), GRAD_TYPES[d]) for d in range(WIN)
    ]
    text_shape = jax.ShapeDtypeStruct(queries.shape, jnp.bfloat16)
    n_in = 4 + len(flat)
    carried = tuple(text)
    offset = 0 if text else 2
    results = pl.pallas_call(
        functools.partial(attend_kernel, sizes, len(carried), (head, at)),
        out_shape=[text_shape, text_shape] + grad_shapes,
        grid=(heads,),
        in_specs=[smem, smem, vmem, vmem]
        + [vmem] * len(flat)
        + [hbm] * len(text),
        out_specs=[text_spec] * 2 + [vmem] * len(grad_shapes),
        scratch_shapes=[
            pltpu.VMEM((WIN, HD, img), jnp.bfloat16),
            pltpu.VMEM((WIN, HD, img), jnp.bfloat16),
            pltpu.VMEM((WIN, img, width), jnp.float32),
            pltpu.VMEM((8, width), jnp.float32),
            pltpu.VMEM((8, width), jnp.float32),
            pltpu.VMEM((1, width), jnp.float32),
            pltpu.VMEM((1, width), jnp.float32),
            pltpu.VMEM((HD, width), jnp.float32),
            pltpu.VMEM((HD, width), jnp.float32),
        ],
        input_output_aliases={n_in + i: i + offset for i in range(len(carried))},
        compiler_params=pltpu.CompilerParams(vmem_limit_bytes=VMEM_LIMIT),
        cost_estimate=pl.CostEstimate(
            flops=heads * WIN * img * tok * GROUP * HD, bytes_accessed=heads * 2**20, transcendentals=0
        ),
    )(spans, gain, queries, grad_out, *flat, *carried)
    return tuple(results[:2]), tuple(results[2:])


def shifted(shard, axis, by):
    count = lax.axis_size(axis)
    pairs = [(i, i + by) for i in range(count) if 0 <= i + by < count]
    return lax.ppermute(shard, axis, pairs)


def rotated(shard, axis, by):
    count = lax.axis_size(axis)
    return lax.ppermute(shard, axis, [(i, (i + by) % count) for i in range(count)])


def exchanged(shard, axis):
    return lax.ppermute(shard, axis, [(i, i ^ 1) for i in range(lax.axis_size(axis))])


def after(values, earlier):
    return lax.optimization_barrier((values, earlier))[0]


def slot_bounds(image_spans, image_owner):
    image_count = image_spans.shape[0]
    owner_match = image_owner[None, :] == jnp.arange(image_count, dtype=jnp.int32)[:, None]
    slot_start = jnp.sum(jnp.where(owner_match, image_spans[None, :, 0], 0), axis=1)
    slot_end = jnp.sum(jnp.where(owner_match, image_spans[None, :, 1], 0), axis=1)
    return (slot_start, slot_end)


def shards(queries, image_kv, image_spans, image_owner, gate_logit, grad_out):
    head_count = lax.axis_size("head")
    my_head = lax.axis_index("head")
    my_shard = lax.axis_index("seq")
    odd = my_shard % 2 == 1
    tok_rows = queries.shape[0]
    rows = image_kv.shape[1]
    kv_local = KVH // head_count
    gain = jnp.tanh(gate_logit)
    slot_start, slot_end = slot_bounds(image_spans, image_owner)
    image_ids = jnp.arange(image_spans.shape[0], dtype=jnp.int32)
    bounds = []
    for distance in range(WIN):
        slot_match = image_ids == my_shard - distance
        for slot in (slot_start, slot_end):
            at = jnp.sum(jnp.where(slot_match, slot - my_shard * tok_rows, 0))
            bounds.append(jnp.clip(at, 0, tok_rows))
    spans = jnp.stack(bounds).astype(jnp.int32)

    count = max(kv_local // 2, 1)
    groups = [list(range(count))] + [[head] for head in range(count, kv_local)]
    whole = [rows * head_count]
    pieces = [rows] * head_count

    def columns(source, owner, first):
        start = (owner * kv_local + first) * HD
        return lax.dynamic_slice_in_dim(source, start, count * HD, axis=2)

    arrivals = []
    before = ()
    for first in range(0, kv_local, count):
        source = after(image_kv, before)
        slices = [
            columns(source, (my_head + by) % head_count, first) for by in range(head_count)
        ]
        if not arrivals:
            own = slices[:1]
            own += [rotated(slices[by], "head", by) for by in range(1, head_count)]
            before = spans
            arrivals.append(own)
        else:
            early = slices
            slices = after(slices, arrivals[0][1:])
            own = slices[:1]
            own += [rotated(slices[by], "head", by) for by in range(1, head_count)]
            arrivals.append(own)
    if len(arrivals) == 1:
        early = ()
    far = [
        shifted(after(piece, (spans, early)) if by else piece, "seq", 2)
        for by, piece in enumerate(arrivals[0])
    ]
    near = [jnp.where(odd, f, o) for f, o in zip(far, arrivals[0])]
    near = jnp.concatenate(after(near, arrivals[-1][1:]), axis=1)
    kv = [arrivals[0], [exchanged(near, "seq")], far]
    if len(arrivals) > 1:
        next_own = jnp.concatenate(arrivals[1], axis=1)
        next_far = shifted(next_own, "seq", 2)

    def finish(result, pending, earlier):
        first, keeping, backs = pending
        totals = [None] * len(backs)
        for p in reversed(range(len(backs))):
            back = after(backs[p], earlier)
            totals[p] = (keeping[p] + back.astype(jnp.float32)).astype(jnp.bfloat16)
        if len(backs) < head_count:
            totals = [totals[0][:, start:stop] for p, start, stop in cuts_of(pieces)]
        waited = totals[-1]
        for by in reversed(range(head_count)):
            total = rotated(totals[by], "head", -by) if by else totals[by]
            at = (((my_head + by) % head_count) * kv_local + first) * HD
            result = lax.dynamic_update_slice_in_dim(result, total, at, axis=2)
        return result, waited

    text = ()
    result = jnp.zeros_like(image_kv)
    hold = ()
    pending = []

    for g, group in enumerate(groups):
        last = g + 1 == len(groups)
        split = last
        cuts = pieces if split else whole
        text, grads = attend(
            after(spans, hold),
            gain,
            queries,
            grad_out,
            kv,
            text,
            group[0],
            group[0] % count,
            len(group),
        )
        kept, near_grad, gone = grads
        if len(pending) == 2:
            result, waited = finish(result, pending.pop(0), near_grad)
            near_grad = after(near_grad, waited)
        near_back = exchanged(near_grad, "seq")
        if last and len(pending) > 0:
            result, waited = finish(result, pending.pop(0), near_grad)
            near_back = after(near_back, waited)
        if g == 0 and len(arrivals) > 1:
            next_own, next_far = after((next_own, next_far), near_grad)
            kv = [[next_own], [exchanged(jnp.where(odd, next_far, next_own), "seq")], [next_far]]
        leaving, backs, keeping = [], [], []
        for p, start, stop in reversed(cuts_of(cuts)):
            near_part = near_back[:, start:stop].astype(jnp.float32)
            leaving.append((gone[:, start:stop] + jnp.where(odd, near_part, 0.0)).astype(jnp.bfloat16))
            keeping.append(kept[:, start:stop] + jnp.where(odd, 0.0, near_part))
            backs.append(shifted(leaving[-1], "seq", -2))
        hold = leaving
        pending.append((group[0], keeping[::-1], backs[::-1]))
    for n, item in enumerate(pending):
        result, waited = finish(result, item, leaving if n + 1 < len(pending) else ())
    attn_output, grad_queries = text
    return (attn_output, grad_queries, result)


def solution(mesh):
    placed = (P("seq", "head"), P(None, ("seq", "head"), None), P(), P(), P(), P("seq", "head"))
    return jax.shard_map(
        shards,
        mesh=mesh,
        in_specs=placed,
        out_specs=(P("seq", "head"), P("seq", "head"), P(None, ("seq", "head"), None)),
        check_vma=False,
    )
```

```python
import functools, math
import jax
import jax.numpy as jnp
from jax import lax
from jax.experimental import pallas as pl
from jax.experimental.pallas import tpu as pltpu
from jax.sharding import PartitionSpec as P

HEADS = 64
KVH = 8
HD = 128
WIN = 3
GROUP = HEADS // KVH
INV_ROOT = 1.0 / math.sqrt(HD)
LOG2E = 1.4426950408889634
NEG = -1e30
BIG = 1e30
VMEM_LIMIT = 36 * 2**20
GRAD_TYPES = (jnp.float32, jnp.bfloat16, jnp.float32)
BLK = 512
UNROLLED = 2
NT = (((1,), (1,)), ((), ()))
NN = (((1,), (0,)), ((), ()))


def dot(a, b, dims=NN):
    return lax.dot_general(a, b, dims, preferred_element_type=jnp.float32)


def cuts_of(sizes):
    starts = [sum(sizes[:p]) for p in range(len(sizes))]
    return [(p, start, start + size) for p, (start, size) in enumerate(zip(starts, sizes))]


def over_blocks(sizes, body):
    for p, start, stop in cuts_of(sizes):
        blk = min(BLK, stop - start)
        if stop - start <= UNROLLED * blk:
            for r in range(0, stop - start, blk):
                body(p, pl.ds(r, blk), pl.ds(start + r, blk))
        else:

            @pl.loop(0, (stop - start) // blk)
            def _(n):
                r = pl.multiple_of(n * blk, blk)
                body(p, pl.ds(r, blk), pl.ds(pl.multiple_of(start + r, blk), blk))


def attend_kernel(sizes, carried, place, *refs):
    head, at = place
    step = pl.program_id(0)
    refs = list(refs)
    spans, gain_ref, q_ref, g_ref = refs[:4]
    del refs[:4]
    kv = [[refs.pop(0) for size in per] for per in sizes]
    del refs[:carried]
    out_ref, dq_ref = refs[:2]
    del refs[:2]
    grads = [refs.pop(0) for d in range(WIN)]
    kt, vt, s, top, total, m_ref, l_ref, o_ref, dqt_ref = refs
    tok = q_ref.shape[0]
    width = GROUP * tok
    gain = gain_ref[0]

    def column(first):
        return pl.ds(pl.multiple_of(first * HD, HD), HD)

    cols = column(at + step)
    slots = column(step)
    text = [column((head + step) * GROUP + g) for g in range(GROUP)]

    q = jnp.concatenate([q_ref[:, cut] for cut in text], axis=0)
    ag = gain * jnp.concatenate([g_ref[:, cut] for cut in text], axis=0).astype(jnp.float32)
    gl = ag.astype(jnp.bfloat16)
    at_tok = lax.rem(lax.broadcasted_iota(jnp.int32, (1, width), 1), tok)
    m_ref[...] = jnp.full_like(m_ref, NEG)
    l_ref[...] = jnp.zeros_like(l_ref)
    o_ref[...] = jnp.zeros_like(o_ref)
    dqt_ref[...] = jnp.zeros_like(dqt_ref)
    active = [spans[2 * d + 1] > spans[2 * d] for d in range(WIN)]
    allowed = [(at_tok >= spans[2 * d]) & (at_tok < spans[2 * d + 1]) for d in range(WIN)]

    for d in range(WIN):

        @pl.when(active[d])
        def _():
            top[...] = jnp.full_like(top, NEG)

            def body(p, rows, image_rows):
                sc = dot(kv[d][p][0, rows, cols], q, NT)
                s[d, image_rows, :] = sc
                top[...] = jnp.maximum(top[...], jnp.max(sc.reshape(-1, 8, width), axis=0))
                kt[d, :, image_rows] = kv[d][p][0, rows, cols].T
                vt[d, :, image_rows] = kv[d][p][1, rows, cols].T

            over_blocks(sizes[d], body)
            highest = jnp.max(top[...], axis=0, keepdims=True)
            m_ref[...] = jnp.maximum(m_ref[...], jnp.where(allowed[d], highest, NEG))

    for d in range(WIN):

        @pl.when(active[d])
        def _():
            shift = jnp.where(allowed[d], m_ref[...] * (INV_ROOT * LOG2E), BIG)
            total[...] = jnp.zeros_like(total)

            def body(p, rows, image_rows):
                e = jnp.exp2(s[d, image_rows, :] * (INV_ROOT * LOG2E) - shift)
                s[d, image_rows, :] = e
                total[...] += jnp.sum(e.reshape(-1, 8, width), axis=0)
                o_ref[...] += dot(vt[d, :, image_rows], e.astype(jnp.bfloat16))

            over_blocks(sizes[d], body)
            l_ref[...] += jnp.sum(total[...], axis=0, keepdims=True)

    l = l_ref[...]
    rl = 1.0 / jnp.where(l > 0, l, 1.0)
    att_t = o_ref[...] * rl
    delta = jnp.sum(ag.T * att_t, axis=0, keepdims=True)
    out = (gain * att_t).T.astype(jnp.bfloat16)
    for g in range(GROUP):
        out_ref[:, g * HD : (g + 1) * HD] = out[g * tok : (g + 1) * tok]

    for d in range(WIN):
        into = grads[d]

        @pl.when(active[d])
        def _():
            def body(p, rows, image_rows):
                dp = dot(kv[d][p][1, rows, cols], gl, NT)
                prob = s[d, image_rows, :] * rl
                ds = (prob * (dp - delta)).astype(jnp.bfloat16)
                into[1, image_rows, slots] = dot(prob.astype(jnp.bfloat16), gl).astype(into.dtype)
                into[0, image_rows, slots] = (dot(ds, q) * INV_ROOT).astype(into.dtype)
                dqt_ref[...] += dot(kt[d, :, image_rows], ds)

            over_blocks(sizes[d], body)

        @pl.when(jnp.logical_not(active[d]))
        def _():
            into[:, :, slots] = jnp.zeros((*into.shape[:2], HD), into.dtype)

    dq = (dqt_ref[...] * INV_ROOT).T.astype(jnp.bfloat16)
    for g in range(GROUP):
        dq_ref[:, g * HD : (g + 1) * HD] = dq[g * tok : (g + 1) * tok]


def attend(spans, gain, queries, grad_out, kv, text, head, at, heads):
    tok = queries.shape[0]
    sizes = [[piece.shape[1] for piece in per] for per in kv]
    img = sum(sizes[0])
    width = GROUP * tok
    flat = [piece for per in kv for piece in per]
    vmem = pl.BlockSpec(memory_space=pltpu.VMEM)
    smem = pl.BlockSpec(memory_space=pltpu.SMEM)
    hbm = pl.BlockSpec(memory_space=pl.ANY)
    text_spec = pl.BlockSpec((tok, GROUP * HD), lambda i: (0, head + i))
    grad_shapes = [
        jax.ShapeDtypeStruct((2, img, heads * HD), GRAD_TYPES[d]) for d in range(WIN)
    ]
    text_shape = jax.ShapeDtypeStruct(queries.shape, jnp.bfloat16)
    n_in = 4 + len(flat)
    carried = tuple(text)
    offset = 0 if text else 2
    results = pl.pallas_call(
        functools.partial(attend_kernel, sizes, len(carried), (head, at)),
        out_shape=[text_shape, text_shape] + grad_shapes,
        grid=(heads,),
        in_specs=[smem, smem, vmem, vmem]
        + [vmem] * len(flat)
        + [hbm] * len(text),
        out_specs=[text_spec] * 2 + [vmem] * len(grad_shapes),
        scratch_shapes=[
            pltpu.VMEM((WIN, HD, img), jnp.bfloat16),
            pltpu.VMEM((WIN, HD, img), jnp.bfloat16),
            pltpu.VMEM((WIN, img, width), jnp.float32),
            pltpu.VMEM((8, width), jnp.float32),
            pltpu.VMEM((8, width), jnp.float32),
            pltpu.VMEM((1, width), jnp.float32),
            pltpu.VMEM((1, width), jnp.float32),
            pltpu.VMEM((HD, width), jnp.float32),
            pltpu.VMEM((HD, width), jnp.float32),
        ],
        input_output_aliases={n_in + i: i + offset for i in range(len(carried))},
        compiler_params=pltpu.CompilerParams(vmem_limit_bytes=VMEM_LIMIT),
        cost_estimate=pl.CostEstimate(flops=1, bytes_accessed=1, transcendentals=0),
    )(spans, gain, queries, grad_out, *flat, *carried)
    return tuple(results[:2]), tuple(results[2:])


def shifted(shard, axis, by):
    count = lax.axis_size(axis)
    pairs = [(i, i + by) for i in range(count) if 0 <= i + by < count]
    return lax.ppermute(shard, axis, pairs)


def rotated(shard, axis, by):
    count = lax.axis_size(axis)
    return lax.ppermute(shard, axis, [(i, (i + by) % count) for i in range(count)])


def exchanged(shard, axis):
    return lax.ppermute(shard, axis, [(i, i ^ 1) for i in range(lax.axis_size(axis))])


def after(values, earlier):
    return lax.optimization_barrier((values, earlier))[0]


def slot_bounds(image_spans, image_owner):
    image_count = image_spans.shape[0]
    owner_match = image_owner[None, :] == jnp.arange(image_count, dtype=jnp.int32)[:, None]
    slot_start = jnp.sum(jnp.where(owner_match, image_spans[None, :, 0], 0), axis=1)
    slot_end = jnp.sum(jnp.where(owner_match, image_spans[None, :, 1], 0), axis=1)
    return (slot_start, slot_end)


def shards(queries, image_kv, image_spans, image_owner, gate_logit, grad_out):
    head_count = lax.axis_size("head")
    my_head = lax.axis_index("head")
    my_shard = lax.axis_index("seq")
    odd = my_shard % 2 == 1
    tok_rows = queries.shape[0]
    rows = image_kv.shape[1]
    kv_local = KVH // head_count
    gain = jnp.tanh(gate_logit)
    slot_start, slot_end = slot_bounds(image_spans, image_owner)
    image_ids = jnp.arange(image_spans.shape[0], dtype=jnp.int32)
    bounds = []
    for distance in range(WIN):
        slot_match = image_ids == my_shard - distance
        for slot in (slot_start, slot_end):
            at = jnp.sum(jnp.where(slot_match, slot - my_shard * tok_rows, 0))
            bounds.append(jnp.clip(at, 0, tok_rows))
    spans = jnp.stack(bounds).astype(jnp.int32)

    count = max(kv_local // 2, 1)
    groups = [list(range(count))] + [[head] for head in range(count, kv_local)]
    whole = [rows * head_count]
    pieces = [rows] * head_count

    def columns(source, owner, first):
        start = (owner * kv_local + first) * HD
        return lax.dynamic_slice_in_dim(source, start, count * HD, axis=2)

    arrivals = []
    before = ()
    for first in range(0, kv_local, count):
        source = after(image_kv, before)
        slices = [
            columns(source, (my_head + by) % head_count, first) for by in range(1, head_count)
        ]
        if not arrivals:
            source = after(image_kv, slices)
        slices = [columns(source, my_head, first)] + slices
        if not arrivals:
            own = slices[:1]
            own += [rotated(slices[by], "head", by) for by in range(1, head_count)]
            before = spans
            arrivals.append(own)
        else:
            early = slices
            slices = after(slices, arrivals[0][1:])
            own = slices[:1]
            own += [rotated(slices[by], "head", by) for by in range(1, head_count)]
            arrivals.append(own)
    if len(arrivals) == 1:
        early = ()
    far = [
        shifted(after(piece, (spans, early)) if by else piece, "seq", 2)
        for by, piece in enumerate(arrivals[0])
    ]
    near = [jnp.where(odd, f, o) for f, o in zip(far, arrivals[0])]
    near = jnp.concatenate(after(near, arrivals[-1][1:]), axis=1)
    kv = [arrivals[0], [exchanged(near, "seq")], far]
    if len(arrivals) > 1:
        next_own = jnp.concatenate(arrivals[1], axis=1)
        next_far = shifted(next_own, "seq", 2)

    def finish(pending, earlier):
        first, keeping, backs = pending
        backs = [after(back, earlier) for back in backs]
        totals = [
            (keep + back.astype(jnp.float32)).astype(jnp.bfloat16)
            for keep, back in zip(keeping, backs)
        ]
        if len(backs) < head_count:
            totals = [totals[0][:, start:stop] for p, start, stop in cuts_of(pieces)]
        placed = []
        for by in reversed(range(head_count)):
            total = rotated(totals[by], "head", -by) if by else totals[by]
            placed.append((total, (((my_head + by) % head_count) * kv_local + first) * HD))
        return placed, totals

    text = ()
    placed = []
    hold = ()
    pending = []

    for g, group in enumerate(groups):
        last = g + 1 == len(groups)
        split = last
        cuts = pieces if split else whole
        text, grads = attend(
            after(spans, hold),
            gain,
            queries,
            grad_out,
            kv,
            text,
            group[0],
            group[0] % count,
            len(group),
        )
        kept, near_grad, gone = grads
        if len(pending) == 2:
            more, waited = finish(pending.pop(0), near_grad)
            placed += more
            near_grad = after(near_grad, waited)
        near_back = exchanged(near_grad, "seq")
        if last and len(pending) > 0:
            more, waited = finish(pending.pop(0), near_grad)
            placed += more
            near_back = after(near_back, waited)
        if g == 0 and len(arrivals) > 1:
            next_own, next_far = after((next_own, next_far), near_grad)
            kv = [[next_own], [exchanged(jnp.where(odd, next_far, next_own), "seq")], [next_far]]
        leaving, backs, keeping = [], [], []
        for p, start, stop in reversed(cuts_of(cuts)):
            near_part = near_back[:, start:stop].astype(jnp.float32)
            leaving.append((gone[:, start:stop] + jnp.where(odd, near_part, 0.0)).astype(jnp.bfloat16))
            keeping.append(kept[:, start:stop] + jnp.where(odd, 0.0, near_part))
            backs.append(shifted(leaving[-1], "seq", -2))
        hold = leaving
        pending.append((group[0], keeping[::-1], backs[::-1]))
    more, waited = finish(pending.pop(), ())
    for item in pending:
        placed += finish(item, leaving)[0]
    result = jnp.zeros_like(image_kv)
    for columns_of, at in [(after(total, waited[-1]), at) for total, at in placed] + more:
        result = lax.dynamic_update_slice_in_dim(result, columns_of, at, axis=2)
    attn_output, grad_queries = text
    return (attn_output, grad_queries, result)


def solution(mesh):
    placed = (P("seq", "head"), P(None, ("seq", "head"), None), P(), P(), P(), P("seq", "head"))
    return jax.shard_map(
        shards,
        mesh=mesh,
        in_specs=placed,
        out_specs=(P("seq", "head"), P("seq", "head"), P(None, ("seq", "head"), None)),
        check_vma=False,
    )
```

```python
import functools, math
import jax
import jax.numpy as jnp
from jax import lax
from jax.experimental import pallas as pl
from jax.experimental.pallas import tpu as pltpu
from jax.sharding import PartitionSpec as P

HEADS = 64
KVH = 8
HD = 128
WIN = 3
GROUP = HEADS // KVH
INV_ROOT = 1.0 / math.sqrt(HD)
LOG2E = 1.4426950408889634
NEG = -1e30
BIG = 1e30
VMEM_LIMIT = 36 * 2**20
GRAD_TYPES = (jnp.float32, jnp.bfloat16, jnp.float32)
BLK = 512
UNROLLED = 2
NT = (((1,), (1,)), ((), ()))
NN = (((1,), (0,)), ((), ()))


def dot(a, b, dims=NN):
    return lax.dot_general(a, b, dims, preferred_element_type=jnp.float32)


def cuts_of(sizes):
    starts = [sum(sizes[:p]) for p in range(len(sizes))]
    return [(p, start, start + size) for p, (start, size) in enumerate(zip(starts, sizes))]


def over_blocks(sizes, body):
    for p, start, stop in cuts_of(sizes):
        blk = min(BLK, stop - start)
        if stop - start <= UNROLLED * blk:
            for r in range(0, stop - start, blk):
                body(p, pl.ds(r, blk), pl.ds(start + r, blk))
        else:

            @pl.loop(0, (stop - start) // blk)
            def _(n):
                r = pl.multiple_of(n * blk, blk)
                body(p, pl.ds(r, blk), pl.ds(pl.multiple_of(start + r, blk), blk))


def attend_kernel(sizes, carried, place, *refs):
    head, at = place
    step = pl.program_id(0)
    refs = list(refs)
    spans, gain_ref, q_ref, g_ref = refs[:4]
    del refs[:4]
    kv = [[refs.pop(0) for size in per] for per in sizes]
    del refs[:carried]
    out_ref, dq_ref = refs[:2]
    del refs[:2]
    grads = [refs.pop(0) for d in range(WIN)]
    kt, vt, s, top, total, m_ref, l_ref, o_ref, dqt_ref = refs
    tok = q_ref.shape[0]
    width = GROUP * tok
    gain = gain_ref[0]

    def column(first):
        return pl.ds(pl.multiple_of(first * HD, HD), HD)

    cols = column(at + step)
    slots = column(step)
    text = [column((head + step) * GROUP + g) for g in range(GROUP)]

    q = jnp.concatenate([q_ref[:, cut] for cut in text], axis=0)
    ag = gain * jnp.concatenate([g_ref[:, cut] for cut in text], axis=0).astype(jnp.float32)
    gl = ag.astype(jnp.bfloat16)
    at_tok = lax.rem(lax.broadcasted_iota(jnp.int32, (1, width), 1), tok)
    m_ref[...] = jnp.full_like(m_ref, NEG)
    l_ref[...] = jnp.zeros_like(l_ref)
    o_ref[...] = jnp.zeros_like(o_ref)
    dqt_ref[...] = jnp.zeros_like(dqt_ref)
    active = [spans[2 * d + 1] > spans[2 * d] for d in range(WIN)]
    allowed = [(at_tok >= spans[2 * d]) & (at_tok < spans[2 * d + 1]) for d in range(WIN)]

    for d in range(WIN):

        @pl.when(active[d])
        def _():
            top[...] = jnp.full_like(top, NEG)

            def body(p, rows, image_rows):
                sc = dot(kv[d][p][0, rows, cols], q, NT)
                s[d, image_rows, :] = sc
                top[...] = jnp.maximum(top[...], jnp.max(sc.reshape(-1, 8, width), axis=0))
                kt[d, :, image_rows] = kv[d][p][0, rows, cols].T
                vt[d, :, image_rows] = kv[d][p][1, rows, cols].T

            over_blocks(sizes[d], body)
            highest = jnp.max(top[...], axis=0, keepdims=True)
            m_ref[...] = jnp.maximum(m_ref[...], jnp.where(allowed[d], highest, NEG))

    for d in range(WIN):

        @pl.when(active[d])
        def _():
            shift = jnp.where(allowed[d], m_ref[...] * (INV_ROOT * LOG2E), BIG)
            total[...] = jnp.zeros_like(total)

            def body(p, rows, image_rows):
                e = jnp.exp2(s[d, image_rows, :] * (INV_ROOT * LOG2E) - shift)
                s[d, image_rows, :] = e
                total[...] += jnp.sum(e.reshape(-1, 8, width), axis=0)
                o_ref[...] += dot(vt[d, :, image_rows], e.astype(jnp.bfloat16))

            over_blocks(sizes[d], body)
            l_ref[...] += jnp.sum(total[...], axis=0, keepdims=True)

    l = l_ref[...]
    rl = 1.0 / jnp.where(l > 0, l, 1.0)
    att_t = o_ref[...] * rl
    delta = jnp.sum(ag.T * att_t, axis=0, keepdims=True)
    out = (gain * att_t).T.astype(jnp.bfloat16)
    for g in range(GROUP):
        out_ref[:, g * HD : (g + 1) * HD] = out[g * tok : (g + 1) * tok]

    for d in range(WIN):
        into = grads[d]

        @pl.when(active[d])
        def _():
            def body(p, rows, image_rows):
                dp = dot(kv[d][p][1, rows, cols], gl, NT)
                prob = s[d, image_rows, :] * rl
                ds = (prob * (dp - delta)).astype(jnp.bfloat16)
                into[1, image_rows, slots] = dot(prob.astype(jnp.bfloat16), gl).astype(into.dtype)
                into[0, image_rows, slots] = (dot(ds, q) * INV_ROOT).astype(into.dtype)
                dqt_ref[...] += dot(kt[d, :, image_rows], ds)

            over_blocks(sizes[d], body)

        @pl.when(jnp.logical_not(active[d]))
        def _():
            into[:, :, slots] = jnp.zeros((*into.shape[:2], HD), into.dtype)

    dq = (dqt_ref[...] * INV_ROOT).T.astype(jnp.bfloat16)
    for g in range(GROUP):
        dq_ref[:, g * HD : (g + 1) * HD] = dq[g * tok : (g + 1) * tok]


def attend(spans, gain, queries, grad_out, kv, text, head, at, heads):
    tok = queries.shape[0]
    sizes = [[piece.shape[1] for piece in per] for per in kv]
    img = sum(sizes[0])
    width = GROUP * tok
    flat = [piece for per in kv for piece in per]
    vmem = pl.BlockSpec(memory_space=pltpu.VMEM)
    smem = pl.BlockSpec(memory_space=pltpu.SMEM)
    hbm = pl.BlockSpec(memory_space=pl.ANY)
    text_spec = pl.BlockSpec((tok, GROUP * HD), lambda i: (0, head + i))
    grad_shapes = [
        jax.ShapeDtypeStruct((2, img, heads * HD), GRAD_TYPES[d]) for d in range(WIN)
    ]
    text_shape = jax.ShapeDtypeStruct(queries.shape, jnp.bfloat16)
    n_in = 4 + len(flat)
    carried = tuple(text)
    offset = 0 if text else 2
    results = pl.pallas_call(
        functools.partial(attend_kernel, sizes, len(carried), (head, at)),
        out_shape=[text_shape, text_shape] + grad_shapes,
        grid=(heads,),
        in_specs=[smem, smem, vmem, vmem]
        + [vmem] * len(flat)
        + [hbm] * len(text),
        out_specs=[text_spec] * 2 + [vmem] * len(grad_shapes),
        scratch_shapes=[
            pltpu.VMEM((WIN, HD, img), jnp.bfloat16),
            pltpu.VMEM((WIN, HD, img), jnp.bfloat16),
            pltpu.VMEM((WIN, img, width), jnp.float32),
            pltpu.VMEM((8, width), jnp.float32),
            pltpu.VMEM((8, width), jnp.float32),
            pltpu.VMEM((1, width), jnp.float32),
            pltpu.VMEM((1, width), jnp.float32),
            pltpu.VMEM((HD, width), jnp.float32),
            pltpu.VMEM((HD, width), jnp.float32),
        ],
        input_output_aliases={n_in + i: i + offset for i in range(len(carried))},
        compiler_params=pltpu.CompilerParams(vmem_limit_bytes=VMEM_LIMIT),
        cost_estimate=pl.CostEstimate(flops=1, bytes_accessed=1, transcendentals=0),
    )(spans, gain, queries, grad_out, *flat, *carried)
    return tuple(results[:2]), tuple(results[2:])


def shifted(shard, axis, by):
    count = lax.axis_size(axis)
    pairs = [(i, i + by) for i in range(count) if 0 <= i + by < count]
    return lax.ppermute(shard, axis, pairs)


def rotated(shard, axis, by):
    count = lax.axis_size(axis)
    return lax.ppermute(shard, axis, [(i, (i + by) % count) for i in range(count)])


def exchanged(shard, axis):
    return lax.ppermute(shard, axis, [(i, i ^ 1) for i in range(lax.axis_size(axis))])


def after(values, earlier):
    return lax.optimization_barrier((values, earlier))[0]


def slot_bounds(image_spans, image_owner):
    image_count = image_spans.shape[0]
    owner_match = image_owner[None, :] == jnp.arange(image_count, dtype=jnp.int32)[:, None]
    slot_start = jnp.sum(jnp.where(owner_match, image_spans[None, :, 0], 0), axis=1)
    slot_end = jnp.sum(jnp.where(owner_match, image_spans[None, :, 1], 0), axis=1)
    return (slot_start, slot_end)


def shards(queries, image_kv, image_spans, image_owner, gate_logit, grad_out):
    head_count = lax.axis_size("head")
    my_head = lax.axis_index("head")
    my_shard = lax.axis_index("seq")
    odd = my_shard % 2 == 1
    tok_rows = queries.shape[0]
    rows = image_kv.shape[1]
    kv_local = KVH // head_count
    gain = jnp.tanh(gate_logit)
    slot_start, slot_end = slot_bounds(image_spans, image_owner)
    image_ids = jnp.arange(image_spans.shape[0], dtype=jnp.int32)
    bounds = []
    for distance in range(WIN):
        slot_match = image_ids == my_shard - distance
        for slot in (slot_start, slot_end):
            at = jnp.sum(jnp.where(slot_match, slot - my_shard * tok_rows, 0))
            bounds.append(jnp.clip(at, 0, tok_rows))
    spans = jnp.stack(bounds).astype(jnp.int32)

    count = max(kv_local // 2, 1)
    groups = [list(range(count))] + [[head] for head in range(count, kv_local)]
    whole = [rows * head_count]
    pieces = [rows] * head_count

    def columns(source, owner, first):
        start = (owner * kv_local + first) * HD
        return lax.dynamic_slice_in_dim(source, start, count * HD, axis=2)

    arrivals = []
    before = ()
    for first in range(0, kv_local, count):
        source = after(image_kv, before)
        slices = [
            columns(source, (my_head + by) % head_count, first) for by in range(1, head_count)
        ]
        if not arrivals:
            source = after(image_kv, slices)
        slices = [columns(source, my_head, first)] + slices
        if not arrivals:
            own = slices[:1]
            own += [rotated(slices[by], "head", by) for by in range(1, head_count)]
            before = spans
            arrivals.append(own)
        else:
            early = slices
            slices = after(slices, arrivals[0][1:])
            own = slices[:1]
            own += [rotated(slices[by], "head", by) for by in range(1, head_count)]
            arrivals.append(own)
    if len(arrivals) == 1:
        early = ()
    far = [
        shifted(after(piece, (spans, early)) if by else piece, "seq", 2)
        for by, piece in enumerate(arrivals[0])
    ]
    near = [jnp.where(odd, f, o) for f, o in zip(far, arrivals[0])]
    near = jnp.concatenate(after(near, arrivals[-1][1:]), axis=1)
    kv = [arrivals[0], [exchanged(near, "seq")], far]
    if len(arrivals) > 1:
        next_own = jnp.concatenate(arrivals[1], axis=1)
        next_far = shifted(next_own, "seq", 2)

    def finish(pending, earlier):
        first, keeping, backs = pending
        backs = [after(back, earlier) for back in backs]
        totals = [
            (keep + back.astype(jnp.float32)).astype(jnp.bfloat16)
            for keep, back in zip(keeping, backs)
        ]
        if len(backs) < head_count:
            totals = [totals[0][:, start:stop] for p, start, stop in cuts_of(pieces)]
        placed = []
        for by in reversed(range(head_count)):
            total = rotated(totals[by], "head", -by) if by else totals[by]
            placed.append((total, (((my_head + by) % head_count) * kv_local + first) * HD))
        return placed, totals

    text = ()
    placed = []
    hold = ()
    pending = []

    for g, group in enumerate(groups):
        last = g + 1 == len(groups)
        split = g > 0
        cuts = pieces if split else whole
        text, grads = attend(
            after(spans, hold),
            gain,
            queries,
            grad_out,
            kv,
            text,
            group[0],
            group[0] % count,
            len(group),
        )
        kept, near_grad, gone = grads
        if len(pending) == 2:
            more, waited = finish(pending.pop(0), near_grad)
            placed += more
            near_grad = after(near_grad, waited)
        near_back = exchanged(near_grad, "seq")
        if last and len(pending) > 0:
            more, waited = finish(pending.pop(0), near_grad)
            placed += more
            near_back = after(near_back, waited[-1])
        if g == 0 and len(arrivals) > 1:
            next_own, next_far = after((next_own, next_far), near_grad)
            kv = [[next_own], [exchanged(jnp.where(odd, next_far, next_own), "seq")], [next_far]]
        leaving, backs, keeping = [], [], []
        for p, start, stop in reversed(cuts_of(cuts)):
            near_part = near_back[:, start:stop].astype(jnp.float32)
            leaving.append((gone[:, start:stop] + jnp.where(odd, near_part, 0.0)).astype(jnp.bfloat16))
            keeping.append(kept[:, start:stop] + jnp.where(odd, 0.0, near_part))
            backs.append(shifted(leaving[-1], "seq", -2))
        hold = leaving
        pending.append((group[0], keeping[::-1], backs[::-1]))
    more, waited = finish(pending.pop(), ())
    for item in pending:
        placed += finish(item, leaving)[0]
    result = jnp.zeros_like(image_kv)
    for columns_of, at in [(after(total, waited[-1]), at) for total, at in placed] + more:
        result = lax.dynamic_update_slice_in_dim(result, columns_of, at, axis=2)
    attn_output, grad_queries = text
    return (attn_output, grad_queries, result)


def solution(mesh):
    placed = (P("seq", "head"), P(None, ("seq", "head"), None), P(), P(), P(), P("seq", "head"))
    return jax.shard_map(
        shards,
        mesh=mesh,
        in_specs=placed,
        out_specs=(P("seq", "head"), P("seq", "head"), P(None, ("seq", "head"), None)),
        check_vma=False,
    )
```

```python
import functools, math
import jax
import jax.numpy as jnp
from jax import lax
from jax.experimental import pallas as pl
from jax.experimental.pallas import tpu as pltpu
from jax.sharding import PartitionSpec as P

HEADS = 64
KVH = 8
HD = 128
WIN = 3
GROUP = HEADS // KVH
INV_ROOT = 1.0 / math.sqrt(HD)
LOG2E = 1.4426950408889634
NEG = -1e30
BIG = 1e30
VMEM_LIMIT = 36 * 2**20
GRAD_TYPES = (jnp.float32, jnp.bfloat16, jnp.float32)
BLK = 1024
UNROLLED = 2
NT = (((1,), (1,)), ((), ()))
NN = (((1,), (0,)), ((), ()))


def dot(a, b, dims=NN):
    return lax.dot_general(a, b, dims, preferred_element_type=jnp.float32)


def cuts_of(sizes):
    starts = [sum(sizes[:p]) for p in range(len(sizes))]
    return [(p, start, start + size) for p, (start, size) in enumerate(zip(starts, sizes))]


def over_blocks(sizes, body):
    for p, start, stop in cuts_of(sizes):
        blk = min(BLK, stop - start)
        if stop - start <= UNROLLED * blk:
            for r in range(0, stop - start, blk):
                body(p, pl.ds(r, blk), pl.ds(start + r, blk))
        else:

            @pl.loop(0, (stop - start) // blk)
            def _(n):
                r = pl.multiple_of(n * blk, blk)
                body(p, pl.ds(r, blk), pl.ds(pl.multiple_of(start + r, blk), blk))


def attend_kernel(sizes, carried, place, *refs):
    head, at = place
    step = pl.program_id(0)
    refs = list(refs)
    spans, gain_ref, q_ref, g_ref = refs[:4]
    del refs[:4]
    kv = [[refs.pop(0) for size in per] for per in sizes]
    del refs[:carried]
    out_ref, dq_ref = refs[:2]
    del refs[:2]
    grads = [refs.pop(0) for d in range(WIN)]
    kt, vt, s, top, total, m_ref, l_ref, o_ref, dqt_ref = refs
    tok = q_ref.shape[0]
    width = GROUP * tok
    gain = gain_ref[0]

    def column(first):
        return pl.ds(pl.multiple_of(first * HD, HD), HD)

    cols = column(at + step)
    slots = column(step)
    text = [column((head + step) * GROUP + g) for g in range(GROUP)]

    q = jnp.concatenate([q_ref[:, cut] for cut in text], axis=0)
    ag = gain * jnp.concatenate([g_ref[:, cut] for cut in text], axis=0).astype(jnp.float32)
    gl = ag.astype(jnp.bfloat16)
    at_tok = lax.rem(lax.broadcasted_iota(jnp.int32, (1, width), 1), tok)
    m_ref[...] = jnp.full_like(m_ref, NEG)
    l_ref[...] = jnp.zeros_like(l_ref)
    o_ref[...] = jnp.zeros_like(o_ref)
    dqt_ref[...] = jnp.zeros_like(dqt_ref)
    active = [spans[2 * d + 1] > spans[2 * d] for d in range(WIN)]
    allowed = [(at_tok >= spans[2 * d]) & (at_tok < spans[2 * d + 1]) for d in range(WIN)]

    for d in range(WIN):

        @pl.when(active[d])
        def _():
            top[...] = jnp.full_like(top, NEG)

            def body(p, rows, image_rows):
                sc = dot(kv[d][p][0, rows, cols], q, NT)
                s[d, image_rows, :] = sc
                top[...] = jnp.maximum(top[...], jnp.max(sc.reshape(-1, 8, width), axis=0))
                kt[d, :, image_rows] = kv[d][p][0, rows, cols].T
                vt[d, :, image_rows] = kv[d][p][1, rows, cols].T

            over_blocks(sizes[d], body)
            highest = jnp.max(top[...], axis=0, keepdims=True)
            m_ref[...] = jnp.maximum(m_ref[...], jnp.where(allowed[d], highest, NEG))

    for d in range(WIN):

        @pl.when(active[d])
        def _():
            shift = jnp.where(allowed[d], m_ref[...] * (INV_ROOT * LOG2E), BIG)
            total[...] = jnp.zeros_like(total)

            def body(p, rows, image_rows):
                e = jnp.exp2(s[d, image_rows, :] * (INV_ROOT * LOG2E) - shift)
                s[d, image_rows, :] = e
                total[...] += jnp.sum(e.reshape(-1, 8, width), axis=0)
                o_ref[...] += dot(vt[d, :, image_rows], e.astype(jnp.bfloat16))

            over_blocks(sizes[d], body)
            l_ref[...] += jnp.sum(total[...], axis=0, keepdims=True)

    l = l_ref[...]
    rl = 1.0 / jnp.where(l > 0, l, 1.0)
    att_t = o_ref[...] * rl
    delta = jnp.sum(ag.T * att_t, axis=0, keepdims=True)
    out = (gain * att_t).T.astype(jnp.bfloat16)
    for g in range(GROUP):
        out_ref[:, g * HD : (g + 1) * HD] = out[g * tok : (g + 1) * tok]

    for d in range(WIN):
        into = grads[d]

        @pl.when(active[d])
        def _():
            def body(p, rows, image_rows):
                dp = dot(kv[d][p][1, rows, cols], gl, NT)
                prob = s[d, image_rows, :] * rl
                ds = (prob * (dp - delta)).astype(jnp.bfloat16)
                into[1, image_rows, slots] = dot(prob.astype(jnp.bfloat16), gl).astype(into.dtype)
                into[0, image_rows, slots] = (dot(ds, q) * INV_ROOT).astype(into.dtype)
                dqt_ref[...] += dot(kt[d, :, image_rows], ds)

            over_blocks(sizes[d], body)

        @pl.when(jnp.logical_not(active[d]))
        def _():
            into[:, :, slots] = jnp.zeros((*into.shape[:2], HD), into.dtype)

    dq = (dqt_ref[...] * INV_ROOT).T.astype(jnp.bfloat16)
    for g in range(GROUP):
        dq_ref[:, g * HD : (g + 1) * HD] = dq[g * tok : (g + 1) * tok]


def attend(spans, gain, queries, grad_out, kv, text, head, at, heads):
    tok = queries.shape[0]
    sizes = [[piece.shape[1] for piece in per] for per in kv]
    img = sum(sizes[0])
    width = GROUP * tok
    flat = [piece for per in kv for piece in per]
    vmem = pl.BlockSpec(memory_space=pltpu.VMEM)
    smem = pl.BlockSpec(memory_space=pltpu.SMEM)
    hbm = pl.BlockSpec(memory_space=pl.ANY)
    text_spec = pl.BlockSpec((tok, GROUP * HD), lambda i: (0, head + i))
    grad_shapes = [
        jax.ShapeDtypeStruct((2, img, heads * HD), GRAD_TYPES[d]) for d in range(WIN)
    ]
    text_shape = jax.ShapeDtypeStruct(queries.shape, jnp.bfloat16)
    n_in = 4 + len(flat)
    carried = tuple(text)
    offset = 0 if text else 2
    results = pl.pallas_call(
        functools.partial(attend_kernel, sizes, len(carried), (head, at)),
        out_shape=[text_shape, text_shape] + grad_shapes,
        grid=(heads,),
        in_specs=[smem, smem, vmem, vmem]
        + [vmem] * len(flat)
        + [hbm] * len(text),
        out_specs=[text_spec] * 2 + [vmem] * len(grad_shapes),
        scratch_shapes=[
            pltpu.VMEM((WIN, HD, img), jnp.bfloat16),
            pltpu.VMEM((WIN, HD, img), jnp.bfloat16),
            pltpu.VMEM((WIN, img, width), jnp.float32),
            pltpu.VMEM((8, width), jnp.float32),
            pltpu.VMEM((8, width), jnp.float32),
            pltpu.VMEM((1, width), jnp.float32),
            pltpu.VMEM((1, width), jnp.float32),
            pltpu.VMEM((HD, width), jnp.float32),
            pltpu.VMEM((HD, width), jnp.float32),
        ],
        input_output_aliases={n_in + i: i + offset for i in range(len(carried))},
        compiler_params=pltpu.CompilerParams(vmem_limit_bytes=VMEM_LIMIT),
        cost_estimate=pl.CostEstimate(flops=1, bytes_accessed=1, transcendentals=0),
    )(spans, gain, queries, grad_out, *flat, *carried)
    return tuple(results[:2]), tuple(results[2:])


def shifted(shard, axis, by):
    count = lax.axis_size(axis)
    pairs = [(i, i + by) for i in range(count) if 0 <= i + by < count]
    return lax.ppermute(shard, axis, pairs)


def rotated(shard, axis, by):
    count = lax.axis_size(axis)
    return lax.ppermute(shard, axis, [(i, (i + by) % count) for i in range(count)])


def exchanged(shard, axis):
    return lax.ppermute(shard, axis, [(i, i ^ 1) for i in range(lax.axis_size(axis))])


def after(values, earlier):
    return lax.optimization_barrier((values, earlier))[0]


def slot_bounds(image_spans, image_owner):
    image_count = image_spans.shape[0]
    owner_match = image_owner[None, :] == jnp.arange(image_count, dtype=jnp.int32)[:, None]
    slot_start = jnp.sum(jnp.where(owner_match, image_spans[None, :, 0], 0), axis=1)
    slot_end = jnp.sum(jnp.where(owner_match, image_spans[None, :, 1], 0), axis=1)
    return (slot_start, slot_end)


def shards(queries, image_kv, image_spans, image_owner, gate_logit, grad_out):
    head_count = lax.axis_size("head")
    my_head = lax.axis_index("head")
    my_shard = lax.axis_index("seq")
    odd = my_shard % 2 == 1
    tok_rows = queries.shape[0]
    rows = image_kv.shape[1]
    kv_local = KVH // head_count
    gain = jnp.tanh(gate_logit)
    slot_start, slot_end = slot_bounds(image_spans, image_owner)
    image_ids = jnp.arange(image_spans.shape[0], dtype=jnp.int32)
    bounds = []
    for distance in range(WIN):
        slot_match = image_ids == my_shard - distance
        for slot in (slot_start, slot_end):
            at = jnp.sum(jnp.where(slot_match, slot - my_shard * tok_rows, 0))
            bounds.append(jnp.clip(at, 0, tok_rows))
    spans = jnp.stack(bounds).astype(jnp.int32)

    count = max(kv_local // 2, 1)
    groups = [list(range(count))] + [[head] for head in range(count, kv_local)]
    whole = [rows * head_count]
    pieces = [rows] * head_count

    def columns(source, owner, first):
        start = (owner * kv_local + first) * HD
        return lax.dynamic_slice_in_dim(source, start, count * HD, axis=2)

    arrivals = []
    before = ()
    for first in range(0, kv_local, count):
        source = after(image_kv, before)
        slices = [
            columns(source, (my_head + by) % head_count, first) for by in range(1, head_count)
        ]
        if not arrivals:
            source = after(image_kv, slices)
        slices = [columns(source, my_head, first)] + slices
        if not arrivals:
            own = slices[:1]
            own += [rotated(slices[by], "head", by) for by in range(1, head_count)]
            before = spans
            arrivals.append(own)
        else:
            early = slices
            slices = after(slices, arrivals[0][1:])
            own = slices[:1]
            own += [rotated(slices[by], "head", by) for by in range(1, head_count)]
            arrivals.append(own)
    if len(arrivals) == 1:
        early = ()
    far = [
        shifted(after(piece, (spans, early)) if by else piece, "seq", 2)
        for by, piece in enumerate(arrivals[0])
    ]
    near = [jnp.where(odd, f, o) for f, o in zip(far, arrivals[0])]
    near = jnp.concatenate(after(near, arrivals[-1][1:]), axis=1)
    kv = [arrivals[0], [exchanged(near, "seq")], far]
    if len(arrivals) > 1:
        next_own = jnp.concatenate(arrivals[1], axis=1)
        next_far = shifted(next_own, "seq", 2)

    def finish(pending, earlier):
        first, keeping, backs = pending
        backs = [after(back, earlier) for back in backs]
        totals = [
            (keep + back.astype(jnp.float32)).astype(jnp.bfloat16)
            for keep, back in zip(keeping, backs)
        ]
        if len(backs) < head_count:
            totals = [totals[0][:, start:stop] for p, start, stop in cuts_of(pieces)]
        placed = []
        for by in reversed(range(head_count)):
            total = rotated(totals[by], "head", -by) if by else totals[by]
            placed.append((total, (((my_head + by) % head_count) * kv_local + first) * HD))
        return placed, totals

    text = ()
    placed = []
    hold = ()
    pending = []

    for g, group in enumerate(groups):
        last = g + 1 == len(groups)
        split = last
        cuts = pieces if split else whole
        text, grads = attend(
            after(spans, hold),
            gain,
            queries,
            grad_out,
            kv,
            text,
            group[0],
            group[0] % count,
            len(group),
        )
        kept, near_grad, gone = grads
        if len(pending) == 2:
            more, waited = finish(pending.pop(0), near_grad)
            placed += more
            near_grad = after(near_grad, waited)
        near_back = exchanged(near_grad, "seq")
        if last and len(pending) > 0:
            more, waited = finish(pending.pop(0), near_grad)
            placed += more
            near_back = after(near_back, waited)
        if g == 0 and len(arrivals) > 1:
            next_own, next_far = after((next_own, next_far), near_grad)
            kv = [[next_own], [exchanged(jnp.where(odd, next_far, next_own), "seq")], [next_far]]
        leaving, backs, keeping = [], [], []
        for p, start, stop in reversed(cuts_of(cuts)):
            near_part = near_back[:, start:stop].astype(jnp.float32)
            leaving.append((gone[:, start:stop] + jnp.where(odd, near_part, 0.0)).astype(jnp.bfloat16))
            keeping.append(kept[:, start:stop] + jnp.where(odd, 0.0, near_part))
            backs.append(shifted(leaving[-1], "seq", -2))
        hold = leaving
        pending.append((group[0], keeping[::-1], backs[::-1]))
    more, waited = finish(pending.pop(), ())
    for item in pending:
        placed += finish(item, leaving)[0]
    result = jnp.zeros_like(image_kv)
    for columns_of, at in [(after(total, waited[-1]), at) for total, at in placed] + more:
        result = lax.dynamic_update_slice_in_dim(result, columns_of, at, axis=2)
    attn_output, grad_queries = text
    return (attn_output, grad_queries, result)


def solution(mesh):
    placed = (P("seq", "head"), P(None, ("seq", "head"), None), P(), P(), P(), P("seq", "head"))
    return jax.shard_map(
        shards,
        mesh=mesh,
        in_specs=placed,
        out_specs=(P("seq", "head"), P("seq", "head"), P(None, ("seq", "head"), None)),
        check_vma=False,
    )
```
